512 devices in a mesh: trip: 64 (over z, x), virt: 8 (over y, core).
Axes of the slice: x: 4, y: 4, z: 16, core: 2. Of those that a mesh axis runs over, the one named last changes fastest.
Arguments:
- virt_integrals: bfloat16 [64, 2048, 4096], P('trip', 'virt'), may hold values from -6 to 6
- pair_amps: bfloat16 [64, 3, 2, 64, 2048], P('trip', None, None, None, 'virt'), may hold values from -0.0048828125 to 0.0048828125
- hole_amps: bfloat16 [64, 304, 4096], P('trip', 'virt'), may hold values from -0.01171875 to 0.01171875
- coulomb_ints: bfloat16 [64, 3, 304, 64], P('trip', None, 'virt'), may hold values from -6 to 6
- exchange_ints: bfloat16 [64, 3, 4096], P('trip'), may hold values from -2.5 to 2.5
- singles: bfloat16 [64, 64], P('trip'), may hold values from -3 to 3
- occ_energy: bfloat16 [64], P('trip'), may hold values from -3 to -0.29882812
- virt_energy: float32 [64], replicated, may hold values from 0.5 to 4
- triples: int32 [128, 3], P('trip'), may hold values from -1 to 63, as said below
Outputs:
- triple_energy: float32 [128, 64], P('trip')
The draws below stay inside these ranges and needn't reach their ends.
Inputs may be any that keep to these rules, and one draw needn't show every extreme that they name: Rows 2 * t to 2 * t + 1 belong to orbital t: the first of them hold distinct triples (i, j, t) with t < j < i <= t + 3, the others hold -1 in all three columns; some orbital has all 2 rows filled.
All inputs are finite; a program needn't handle non-finite values.
Results may differ from the reference program's by a relative error of at most 0.0025.
Values may be sent and summed in bfloat16 or wider, within the bound.
No kernel may reach another device: no remote copies, remote signals or barrier semaphores. Data moves between devices by JAX's collectives and lax.ppermute only.
A program may use at most 128 MiB of HBM per device.

```python
import jax
import jax.numpy as jnp
import numpy as np
from jax import lax

NV = 2048
NO = 304
NW = 64
REACH = 3
TRIP_MAX = 2
OCC = 64
N_VIRT = 8


def draw_triples(key, part):
    key = jax.random.fold_in(key, 11)
    key_load = jax.random.fold_in(key, 1)
    key_peak = jax.random.fold_in(key, 2)
    key_rank = jax.random.fold_in(key, 3)
    pair_table = np.array([(inner, outer) for outer in range(1, REACH + 1) for inner in range(1, outer)], dtype=np.int32)
    option_count = pair_table.shape[0]
    table_dev = jnp.asarray(pair_table)
    owners = jnp.arange(OCC, dtype=jnp.int32)
    load_level = jax.random.randint(key_load, (OCC,), 0, 16)
    wanted = jnp.where(load_level < 2, 6, jnp.where(load_level < 3, 5, jnp.where(load_level < 5, 4, jnp.where(load_level < 7, 3, jnp.where(load_level < 10, 2, 1)))))
    peak_owner = jax.random.randint(key_peak, (), 0, OCC - REACH)
    wanted = jnp.where(owners == peak_owner, TRIP_MAX, jnp.minimum(wanted, TRIP_MAX))
    usable = owners[:, None] + table_dev[None, :, 1] <= OCC - 1
    live_count = jnp.minimum(wanted, jnp.sum(usable.astype(jnp.int32), axis=1))
    scores = jax.random.randint(key_rank, (OCC, option_count), 0, 1 << 20) * option_count + jnp.arange(option_count)[None, :]
    scores = scores + (1 - usable.astype(jnp.int32)) * (1 << 28)
    ranking = jnp.argsort(scores, axis=1)
    chosen = table_dev[ranking]
    rows_filled = jnp.arange(option_count)[None, :] < live_count[:, None]
    owner_grid = jnp.broadcast_to(owners[:, None], (OCC, option_count))
    triple_rows = jnp.stack([owner_grid + chosen[:, :, 1], owner_grid + chosen[:, :, 0], owner_grid], axis=-1)
    triple_rows = jnp.where(rows_filled[:, :, None], triple_rows, -1)
    return triple_rows[:, :TRIP_MAX].reshape(OCC * TRIP_MAX, 3).astype(jnp.int32)


def shard_levels(stream_key, dims, shards, least, largest):
    gain, own = 1.0, jax.random.fold_in(stream_key, 6)
    for axis_at, shards_of in shards:
        steps = jnp.exp(jax.random.uniform(jax.random.fold_in(own, axis_at), (shards_of,), jnp.float32, least / len(shards), largest / len(shards)))
        gain = gain * jnp.repeat(steps, dims[axis_at] // shards_of).reshape([-1 if axis == axis_at else 1 for axis in range(len(dims))])
    return gain


def scatter_about(stream_key, dims, deviation, most, shards=(), kind=jnp.bfloat16):
    values = jax.random.normal(stream_key, dims, jnp.float32) * deviation
    if len(shards) > 0:
        values = shard_levels(stream_key, dims, shards, -0.22, 0.18) * values
    return jnp.clip(values, min=-most, max=most).astype(kind)


def setup_inputs(seed: int = 0) -> dict:
    key_list = jax.random.split(jax.random.key(seed), 10)
    return {
        "virt_integrals": scatter_about(key_list[0], (OCC, NV, NW * NW), 1.0, 6.0, ((0, 64), (1, 8))),
        "pair_amps": scatter_about(key_list[1], (OCC, REACH, 2, NW, NV), (NV * 816) ** -0.5, 0.0048828125, ((0, 64), (4, 8))),
        "hole_amps": scatter_about(key_list[2], (OCC, NO, NW * NW), (NO * 816) ** -0.5, 0.01171875, ((0, 64), (1, 8))),
        "coulomb_ints": scatter_about(key_list[3], (OCC, REACH, NO, NW), 1.0, 6.0, ((0, 64), (2, 8))),
        "exchange_ints": scatter_about(key_list[4], (OCC, REACH, NW * NW), 0.175, 2.5, ((0, 64),)),
        "singles": scatter_about(key_list[5], (OCC, NW), 0.2, 3.0, ((0, 64),)),
        "occ_energy": jnp.clip(-3.0 + 2.7011719 * jax.random.uniform(key_list[6], (OCC,), jnp.float32) ** shard_levels(key_list[6], (OCC,), ((0, 64),), -0.2, 0.2), -3.0, -0.29882812).astype(jnp.bfloat16),
        "virt_energy": jnp.clip(jax.random.uniform(key_list[7], (NW,), jnp.float32, 0.5, 4.0), 0.5, 4.0),
        "triples": draw_triples(jax.random.fold_in(key_list[9], 71), 0),
    }


AXIS_ORDERS = ((0, 1, 2), (0, 2, 1), (1, 2, 0), (2, 1, 0), (2, 0, 1), (1, 0, 2))


def pair_pick(pair_amps, first_orb, second_orb):
    lower_orb = jnp.minimum(first_orb, second_orb)
    return pair_amps[lower_orb, jnp.abs(first_orb - second_orb) - 1, (first_orb > second_orb).astype(jnp.int32)]


def triple_row(chosen, virt_integrals, pair_amps, hole_amps, coulomb_ints, exchange_ints, singles, occ_energy, virt_energy):
    orb_i, orb_j, orb_k = chosen[0], chosen[1], chosen[2]
    orderings = ((orb_i, orb_j, orb_k), (orb_i, orb_k, orb_j), (orb_k, orb_i, orb_j),
                 (orb_k, orb_j, orb_i), (orb_j, orb_k, orb_i), (orb_j, orb_i, orb_k))
    virt_block = NV // N_VIRT
    occ_block = NO // N_VIRT
    summed = jnp.zeros((NW, NW, NW), jnp.float32)
    for block_index in range(N_VIRT):
        virt_lo = block_index * virt_block
        occ_lo = block_index * occ_block
        partial_value = jnp.zeros((NW, NW, NW), jnp.float32)
        for (lead_orb, mid_orb, third_orb), axes_order in zip(orderings, AXIS_ORDERS):
            amplitudes = pair_pick(pair_amps, lead_orb, mid_orb)[:, virt_lo:virt_lo + virt_block]
            panel_rows = virt_integrals[third_orb, virt_lo:virt_lo + virt_block]
            first_term = jnp.dot(amplitudes.astype(jnp.float32), panel_rows.astype(jnp.float32),
                                 precision=lax.Precision.HIGHEST, preferred_element_type=jnp.float32)
            hole_rows = hole_amps[lead_orb, occ_lo:occ_lo + occ_block]
            coulomb = coulomb_ints[jnp.minimum(mid_orb, third_orb), jnp.abs(mid_orb - third_orb) - 1, occ_lo:occ_lo + occ_block]
            second_term = jnp.einsum("lm,lz->mz", hole_rows.astype(jnp.float32), coulomb.astype(jnp.float32),
                                     precision=lax.Precision.HIGHEST)
            term_block = first_term.reshape(NW, NW, NW) - second_term.reshape(NW, NW, NW)
            partial_value = partial_value + jnp.transpose(term_block, axes_order)
        summed = summed + lax.optimization_barrier(partial_value.astype(jnp.bfloat16)).astype(jnp.float32)
    exch_kj = exchange_ints[orb_k, orb_j - orb_k - 1].astype(jnp.float32).reshape(NW, NW)
    exch_ki = exchange_ints[orb_k, orb_i - orb_k - 1].astype(jnp.float32).reshape(NW, NW)
    exch_ji = exchange_ints[orb_j, orb_i - orb_j - 1].astype(jnp.float32).reshape(NW, NW)
    single_i = singles[orb_i].astype(jnp.float32)
    single_j = singles[orb_j].astype(jnp.float32)
    single_k = singles[orb_k].astype(jnp.float32)
    full_v = (summed + single_i[:, None, None] * exch_kj.T[None, :, :]
              + single_j[None, :, None] * exch_ki.T[:, None, :]
              + single_k[None, None, :] * exch_ji.T[:, :, None])
    cross = 4.0 * summed + jnp.transpose(summed, (2, 0, 1)) + jnp.transpose(summed, (1, 2, 0))
    occ_sum = occ_energy[orb_i].astype(jnp.float32) + occ_energy[orb_j].astype(jnp.float32) + occ_energy[orb_k].astype(jnp.float32)
    denom = occ_sum - virt_energy[:, None, None] - virt_energy[None, :, None] - virt_energy[None, None, :]
    return jnp.sum(cross * (full_v - jnp.transpose(full_v, (2, 1, 0))) / denom, axis=(1, 2))


def reference(virt_integrals, pair_amps, hole_amps, coulomb_ints, exchange_ints, singles, occ_energy, virt_energy, triples):
    def one_row(chosen):
        usable = chosen[0] >= 0
        safe_row = jnp.where(usable, chosen, jnp.array([2, 1, 0], dtype=jnp.int32))
        return lax.cond(usable,
                        lambda picked: triple_row(picked, virt_integrals, pair_amps, hole_amps, coulomb_ints,
                                                  exchange_ints, singles, occ_energy, virt_energy),
                        lambda picked: jnp.zeros((NW,), jnp.float32),
                        safe_row)
    return lax.map(one_row, triples)
```

```python
import jax
import jax.numpy as jnp
from jax import lax
from jax.experimental import pallas as pl
from jax.experimental.pallas import tpu as pltpu
from jax.sharding import PartitionSpec as P

T = 64
H = 32
F32 = jnp.float32
BF16 = jnp.bfloat16
CROWS = 16
BLOCK_ROWS = 2 * T + CROWS
VMEM_LIMIT = 48 * 1024 * 1024


def shift_route(size, distance):
    return [(i, i + distance) for i in range(size) if 0 <= i + distance < size]


def ring_route(step):
    return [(i, (i + 2 * step) % 8) for i in range(8)]


CORE_ROUTE = [(i, i ^ 1) for i in range(8)]


def lane_low(rows):
    return lax.broadcasted_iota(jnp.int32, (rows, 2 * T), 1) < T


def swap_halves(x):
    return jnp.concatenate([x[:, T:], x[:, :T]], axis=1)


def pack_rows(rows64):
    low = lane_low(H)
    top, bottom = rows64[:H], rows64[H:]
    first = jnp.where(low, top, swap_halves(bottom))
    second = jnp.where(low, swap_halves(top), bottom)
    return first, second


def terms_kernel(place, blocks, panels, holes, out):
    y = place[0]
    amps_lead, amps_dup, coul_lead, coul_dup = [], [], [], []
    for d in range(4):
        block = blocks[d]
        second = block[T : 2 * T]
        amps_lead.append(block[:T])
        amps_dup += [second, second]
        packed = block[2 * T :]
        coulomb = jnp.concatenate(
            [packed[:, g * T : (g + 1) * T] for g in range(4)], axis=0
        )
        coul_lead.append(coulomb)
        coul_dup += [coulomb, coulomb]
    amps_lead = jnp.concatenate(amps_lead, axis=0)
    amps_dup = jnp.concatenate(amps_dup, axis=0)
    coul_lead = jnp.concatenate(coul_lead, axis=0)
    coul_dup = jnp.concatenate(coul_dup, axis=0)
    low = lane_low(T)
    contract = (((1,), (1,)), ((), ()))

    def group(step, _):
        rows = pl.ds(pl.multiple_of(step * 8 * T, 8 * T), 8 * T)
        panel = panels[rows, :]
        hole = holes[rows, :]
        by_rows = lax.dot_general(panel, amps_dup, contract, preferred_element_type=F32)
        by_rows += lax.dot_general(hole, coul_dup, contract, preferred_element_type=F32)
        by_cols = lax.dot_general(amps_lead, panel, contract, preferred_element_type=F32)
        by_cols += lax.dot_general(coul_lead, hole, contract, preferred_element_type=F32)
        own = lax.rem(step // 2 - y + 4, 4)
        for pair in range(4):
            row = pair * 2 * T
            for d in range(4):
                col = d * 2 * T
                tile = jnp.where(
                    low,
                    by_rows[row : row + T, col : col + 2 * T],
                    by_rows[row + T : row + 2 * T, col : col + 2 * T],
                )
                tile += by_cols[d * T : (d + 1) * T, row : row + 2 * T]
                if d == 0:
                    at = pl.multiple_of((lax.rem(step, 2) * 4 + pair) * T, T)
                    out[own, 0, pl.ds(at, T), :] = tile.astype(BF16)
                else:
                    at = pl.multiple_of((step * 4 + pair) * 16, 16)
                    for quarter in range(4):
                        rows16 = jnp.concatenate(
                            [
                                tile[8 * quarter : 8 * quarter + 8],
                                tile[H + 8 * quarter : H + 8 * quarter + 8],
                            ],
                            axis=0,
                        )
                        out[lax.rem(quarter - y + 4, 4), d, pl.ds(at, 16), :] = rows16.astype(BF16)
        return 0

    lax.fori_loop(0, 8, group, 0)


def terms(place, blocks, panels, holes):
    vmem = pl.BlockSpec(memory_space=pltpu.VMEM)
    return pl.pallas_call(
        terms_kernel,
        out_shape=jax.ShapeDtypeStruct((4, 4, 512, 2 * T), BF16),
        in_specs=[pl.BlockSpec(memory_space=pltpu.SMEM), vmem, vmem, vmem],
        out_specs=vmem,
        compiler_params=pltpu.CompilerParams(vmem_limit_bytes=VMEM_LIMIT),
        cost_estimate=pl.CostEstimate(
            flops=2 * 4096 * 320 * 768, bytes_accessed=5 << 20, transcendentals=0
        ),
        name="terms",
    )(place, blocks, panels, holes)


def combine_kernel(role, own, one, two, three, out, scratch):
    for index, part in enumerate((one, two, three)):
        scratch[index * 512 : (index + 1) * 512, :] = part[...].astype(F32)
    mid_is_j = jnp.full((T, 2 * T), role[0], jnp.int32) == 1

    def as_rows(index, cp):
        low_rows = scratch[pl.ds(index * 512 + cp, H, stride=16), :]
        high_rows = scratch[pl.ds(index * 512 + 8 + cp, H, stride=16), :]
        low = lane_low(H)
        top = jnp.where(low, low_rows, swap_halves(high_rows))
        bottom = jnp.where(low, swap_halves(low_rows), high_rows)
        return jnp.concatenate([top, bottom], axis=0)

    def turned(x):
        flat = x.T
        return jnp.concatenate([flat[:T], flat[T:]], axis=1)

    for cp in range(8):
        total = own[cp * T : (cp + 1) * T, :].astype(F32)
        total += as_rows(0, cp)
        middle = as_rows(1, cp)
        total += jnp.where(mid_is_j, middle, turned(middle))
        total += turned(as_rows(2, cp))
        out[cp * T : (cp + 1) * T, :] = total.astype(BF16)


def combine(role, own, one, two, three):
    vmem = pl.BlockSpec(memory_space=pltpu.VMEM)
    return pl.pallas_call(
        combine_kernel,
        out_shape=jax.ShapeDtypeStruct((512, 2 * T), BF16),
        in_specs=[pl.BlockSpec(memory_space=pltpu.SMEM)] + [vmem] * 4,
        out_specs=vmem,
        scratch_shapes=[pltpu.VMEM((3 * 512, 2 * T), F32)],
        compiler_params=pltpu.CompilerParams(vmem_limit_bytes=VMEM_LIMIT),
        name="combine",
    )(role, own, one, two, three)


def energy_kernel(place, w0, w1, w2, w3, extra_a, extra_b, inverse, out, whole, flipped, acc, rows_b):
    y = place[0]
    for j, part in enumerate((w0, w1, w2, w3)):
        at = pl.multiple_of(lax.rem(y - j + 4, 4) * 512, 512)
        whole[pl.ds(at, 512), :] = part[...].astype(F32)

    def flip(b, _):
        across = whole[pl.ds(b, H, stride=T), :].T
        flipped[pl.ds(pl.multiple_of(b * H, H), H), :] = jnp.concatenate(
            [across[0:H], across[T : T + H], across[H:T], across[T + H :]], axis=1
        )
        return 0

    lax.fori_loop(0, T, flip, 0, unroll=4)
    acc[...] = jnp.zeros_like(acc)

    def pair(bp, _):
        from_flipped = pack_rows(flipped[pl.ds(bp, T, stride=H), :])
        from_whole = pack_rows(whole[pl.ds(pl.multiple_of(bp * T, T), T), :])
        for half in range(2):
            b = bp + H * half
            at = pl.ds(pl.multiple_of(b * H, H), H)
            plain = whole[pl.ds(b, H, stride=T), :]
            turned = flipped[at, :]
            inv = inverse[at, :]
            first = (4.0 * plain + from_flipped[half]) * (plain - turned + extra_a[at, :]) * inv
            second = plain * (from_flipped[half] - from_whole[half] + extra_b[at, :]) * inv
            acc[...] += first
            rows_b[pl.ds(b, 1), :] = jnp.sum(second, axis=0, keepdims=True)
        return 0

    lax.fori_loop(0, H, pair, 0, unroll=2)
    by_a = jnp.sum(acc[...], axis=0, keepdims=True)
    by_a = by_a[:, :T] + by_a[:, T:]
    by_b = jnp.sum(rows_b[...].T, axis=0, keepdims=True)
    out[...] = jnp.broadcast_to(by_a + by_b, (8, T))


def energy_of(place, parts, extra_a, extra_b, inverse):
    vmem = pl.BlockSpec(memory_space=pltpu.VMEM)
    return pl.pallas_call(
        energy_kernel,
        out_shape=jax.ShapeDtypeStruct((8, T), F32),
        in_specs=[pl.BlockSpec(memory_space=pltpu.SMEM)] + [vmem] * 7,
        out_specs=vmem,
        scratch_shapes=[
            pltpu.VMEM((H * T, 2 * T), F32),
            pltpu.VMEM((H * T, 2 * T), F32),
            pltpu.VMEM((H, 2 * T), F32),
            pltpu.VMEM((T, 2 * T), F32),
        ],
        compiler_params=pltpu.CompilerParams(vmem_limit_bytes=VMEM_LIMIT),
        name="energy",
    )(place, *parts, extra_a, extra_b, inverse)


def pair_blocks(pair_amps, coulomb_ints):
    amps = pair_amps[0].reshape(3, 2 * T, 256)
    coulomb = -jnp.swapaxes(coulomb_ints[0], 1, 2)
    coulomb = jnp.pad(coulomb, ((0, 0), (0, 0), (0, T - coulomb.shape[2])))
    coulomb = coulomb.reshape(3, 4, CROWS, T).transpose(0, 2, 1, 3).reshape(3, CROWS, 4 * T)
    return jnp.concatenate([amps, coulomb], axis=1)


def energy_tables(offset_i, offset_j, usable, exch_kj, exch_ki, exch_ji, singles, occ, virt_energy):
    def pick(table, offset):
        return jnp.sum(
            jnp.where((jnp.arange(4) == offset).reshape((4,) + (1,) * (table.ndim - 1)), table, 0),
            axis=0,
        )

    s_i, s_j, s_k = pick(singles, offset_i), pick(singles, offset_j), singles[0]
    occ_sum = pick(occ, offset_i) + pick(occ, offset_j) + occ[0]
    lanes = 2 * T

    def over_a(v):
        return jnp.tile(v, 2)[None, None, :]

    def over_b(v):
        return v[:, None, None]

    def over_c(v):
        return jnp.concatenate(
            [jnp.broadcast_to(v[:H, None], (H, T)), jnp.broadcast_to(v[H:, None], (H, T))], axis=1
        )[None]

    def over_ca(m):
        return jnp.concatenate([m[:H], m[H:]], axis=1)[None]

    def over_ba(m):
        return jnp.tile(m, (1, 2))[:, None, :]

    def over_bc(m):
        low = jnp.broadcast_to(m[:, :H, None], (T, H, T))
        high = jnp.broadcast_to(m[:, H:, None], (T, H, T))
        return jnp.concatenate([low, high], axis=2)

    extra_a = (
        over_a(s_i) * over_bc(exch_kj.T)
        - over_c(s_i) * over_ba(exch_kj.T)
        + over_b(s_j) * over_ca(exch_ki - exch_ki.T)
        + over_c(s_k) * over_ba(exch_ji)
        - over_a(s_k) * over_bc(exch_ji)
    )
    extra_b = (
        over_b(s_i) * over_ca(exch_kj.T)
        - over_a(s_i) * over_bc(exch_kj)
        + over_c(s_j) * (over_ba(exch_ki.T) - over_ba(exch_ki))
        + over_a(s_k) * over_bc(exch_ji.T)
        - over_b(s_k) * over_ca(exch_ji)
    )
    denom = occ_sum - over_a(virt_energy) - over_b(virt_energy) - over_c(virt_energy)
    inverse = 1.0 / denom
    shape = (H * T, lanes)
    return extra_a.reshape(shape), extra_b.reshape(shape), inverse.reshape(shape)


def local(
    virt_integrals,
    pair_amps,
    hole_amps,
    coulomb_ints,
    exchange_ints,
    singles,
    occ_energy,
    virt_energy,
    triples,
):
    owner = lax.axis_index("trip")
    virt = lax.axis_index("virt")
    n_trip = lax.axis_size("trip")
    y, core = virt // 2, virt % 2
    place = jnp.stack([y, core]).astype(jnp.int32)

    usable = triples[:, 0] >= 0
    off_i = jnp.where(usable, triples[:, 0] - owner, 2)
    off_j = jnp.where(usable, triples[:, 1] - owner, 1)

    def by_core(pairs):
        return jnp.where(core == 0, pairs, pairs[::-1])

    usable, off_i, off_j = by_core(usable), by_core(off_i), by_core(off_j)

    blocks = pair_blocks(pair_amps, coulomb_ints)
    zero = jnp.zeros((), BF16)

    def choose(options, index, live):
        result = jnp.zeros_like(options[0])
        for at, option in enumerate(options):
            result = jnp.where(live & (index == at), option, result)
        return result

    outgoing = []
    for d in (1, 2, 3):
        rows = []
        for s in range(2):
            takes_part = usable[s] & ((off_i[s] == d) | (off_j[s] == d))
            other = off_i[s] + off_j[s] - d
            rows.append(choose([blocks[0], blocks[1], blocks[2]], other - 1, takes_part))
        outgoing.append(jnp.stack(rows))
    exchange = exchange_ints[0].reshape(3, 16, 256)
    small = jnp.concatenate(
        [singles[0], occ_energy, jnp.zeros((16 * 256 - T - 1,), BF16)]
    ).reshape(16, 256)
    from_one = jnp.concatenate([blocks[0], blocks[1], exchange[0], exchange[1], small], axis=0)
    from_two = jnp.concatenate([blocks[0], exchange[0], small], axis=0)

    incoming = [
        lax.ppermute(outgoing[d - 1], "trip", shift_route(n_trip, d)) for d in (1, 2, 3)
    ]
    got_one = lax.ppermute(from_one, "trip", shift_route(n_trip, -1))
    got_two = lax.ppermute(from_two, "trip", shift_route(n_trip, -2))
    got_three = lax.ppermute(small, "trip", shift_route(n_trip, -3))

    panels = virt_integrals[0].reshape(256, T, 2, H).transpose(3, 2, 1, 0).reshape(T * T, 256)
    holes = hole_amps[0].reshape(-1, 2, H, T).transpose(2, 1, 3, 0).reshape(T * T, -1)
    holes = jnp.pad(holes, ((0, 0), (0, T - holes.shape[1])))

    own_options = [got_one[:BLOCK_ROWS], got_one[BLOCK_ROWS : 2 * BLOCK_ROWS], got_two[:BLOCK_ROWS]]

    def own_block(s):
        return choose(own_options, off_i[s] + off_j[s] - 3, usable[s])

    def slots(s):
        return jnp.stack([own_block(s)] + [incoming[d][s] for d in range(3)])

    send = terms(place, slots(1), panels, holes)
    got = lax.ppermute(send, "virt", CORE_ROUTE)
    keep = terms(place, slots(0), panels, holes)
    sums = [(keep[j].astype(F32) + got[j].astype(F32)) for j in range(4)]

    arrived = [
        lax.ppermute(sums[j].astype(BF16), "virt", ring_route(j)) for j in (1, 2, 3)
    ]
    total = sums[0] + arrived[0].astype(F32) + arrived[1].astype(F32) + arrived[2].astype(F32)

    shares = [
        lax.ppermute(total[d].astype(BF16), "trip", shift_route(n_trip, -d)) for d in (1, 2, 3)
    ]
    role = (off_j[0] == 2).astype(jnp.int32).reshape(1)
    chunk = combine(role, total[0], shares[0], shares[1], shares[2])
    parts = [chunk] + [lax.ppermute(chunk, "virt", ring_route(j)) for j in (1, 2, 3)]

    exch_own = exchange_ints[0].astype(F32).reshape(3, T, T)

    def matrix(rows):
        return rows.astype(F32).reshape(T, T)

    first_exch = 2 * BLOCK_ROWS
    exch_ji = choose(
        [
            matrix(got_one[first_exch : first_exch + 16]),
            matrix(got_one[first_exch + 16 : first_exch + 32]),
            matrix(got_two[BLOCK_ROWS : BLOCK_ROWS + 16]),
        ],
        off_i[0] + off_j[0] - 3,
        usable[0],
    )
    exch_kj = choose([exch_own[0], exch_own[1]], off_j[0] - 1, usable[0])
    exch_ki = choose([exch_own[1], exch_own[2]], off_i[0] - 2, usable[0])
    smalls = [small, got_one[first_exch + 32 :], got_two[BLOCK_ROWS + 16 :], got_three]
    singles_by = jnp.stack([x[0, :T].astype(F32) for x in smalls])
    occ_by = jnp.stack([x[0, T].astype(F32) for x in smalls])
    extra_a, extra_b, inverse = energy_tables(
        off_i[0], off_j[0], usable[0], exch_kj, exch_ki, exch_ji, singles_by, occ_by, virt_energy
    )

    mine = energy_of(place, parts, extra_a, extra_b, inverse)[0]
    mine = jnp.where(usable[0], mine, jnp.zeros_like(mine))
    other = lax.ppermute(mine, "virt", CORE_ROUTE)
    return jnp.where(core == 0, jnp.stack([mine, other]), jnp.stack([other, mine]))


def solution(mesh):
    placed = (
        P("trip", "virt", None),
        P("trip", None, None, None, "virt"),
        P("trip", "virt", None),
        P("trip", None, "virt", None),
        P("trip", None, None),
        P("trip", None),
        P("trip"),
        P(),
        P("trip", None),
    )
    return jax.shard_map(
        local, mesh=mesh, in_specs=placed, out_specs=P("trip", None), check_vma=False
    )
```

```python
import functools

import jax
import jax.numpy as jnp
from jax import lax
from jax.experimental import pallas as pl
from jax.experimental.pallas import tpu as pltpu
from jax.sharding import PartitionSpec as P

T = 64
H = 32
F32 = jnp.float32
BF16 = jnp.bfloat16
CROWS = 16
BLOCK_ROWS = 2 * T + CROWS
VMEM_LIMIT = 48 * 1024 * 1024


def shift_route(size, distance):
    return [(i, i + distance) for i in range(size) if 0 <= i + distance < size]


def ring_route(step):
    return [(i, (i + 2 * step) % 8) for i in range(8)]


CORE_ROUTE = [(i, i ^ 1) for i in range(8)]


def lane_low(rows):
    return lax.broadcasted_iota(jnp.int32, (rows, 2 * T), 1) < T


def swap_halves(x):
    return jnp.concatenate([x[:, T:], x[:, :T]], axis=1)


def pack_rows(rows64):
    low = lane_low(H)
    top, bottom = rows64[:H], rows64[H:]
    first = jnp.where(low, top, swap_halves(bottom))
    second = jnp.where(low, swap_halves(top), bottom)
    return first, second


def row_of(triples, owner, core, rel):
    s = jnp.where(core == 0, rel, 1 - rel)
    live = triples[s, 0] >= 0
    off_i = jnp.where(live, triples[s, 0] - owner, 2)
    off_j = jnp.where(live, triples[s, 1] - owner, 1)
    return off_i, off_j, live


def prep_kernel(triples, amps, coulomb, out1, out2, out3, up1, up2, blocks):
    owner, core = lax.axis_index("trip"), lax.rem(lax.axis_index("virt"), 2)
    occ_rows = coulomb.shape[1]
    for s in range(3):
        blocks[s, : 2 * T, :] = amps[s]
        turned = jnp.concatenate(
            [coulomb[s].astype(F32), jnp.zeros((T - occ_rows, T), F32)], axis=0
        ).T
        packed = jnp.concatenate([-turned[g * CROWS : (g + 1) * CROWS] for g in range(4)], axis=1)
        blocks[s, 2 * T :, :] = packed.astype(BF16)
    up1[...] = blocks[0:2]
    up2[...] = blocks[0]
    for rel in range(2):
        off_i, off_j, live = row_of(triples, owner, core, rel)
        for d, out in ((1, out1), (2, out2), (3, out3)):
            takes_part = live & ((off_i == d) | (off_j == d))
            other = jnp.clip(off_i + off_j - d - 1, 0, 2)

            @pl.when(takes_part)
            def _():
                out[rel] = blocks[other]

            @pl.when(jnp.logical_not(takes_part))
            def _():
                out[rel] = jnp.zeros((BLOCK_ROWS, 4 * T), BF16)


def prep(triples, amps, coulomb):
    vmem = pl.BlockSpec(memory_space=pltpu.VMEM)
    two = jax.ShapeDtypeStruct((2, BLOCK_ROWS, 4 * T), BF16)
    one = jax.ShapeDtypeStruct((BLOCK_ROWS, 4 * T), BF16)
    return pl.pallas_call(
        prep_kernel,
        out_shape=(two, two, two, two, one),
        in_specs=[pl.BlockSpec(memory_space=pltpu.SMEM), vmem, vmem],
        out_specs=[vmem] * 5,
        scratch_shapes=[pltpu.VMEM((3, BLOCK_ROWS, 4 * T), BF16)],
        compiler_params=pltpu.CompilerParams(vmem_limit_bytes=VMEM_LIMIT),
        name="prep",
    )(triples, amps, coulomb)


def panels_kernel(integrals, holes, panels_out, holes_out, spread_a, spread_b):
    occ_rows = holes.shape[0]

    def one_chunk(chunk, _):
        columns = pl.ds(pl.multiple_of(chunk * 2 * T, 2 * T), 2 * T)
        turned = integrals[:, columns].astype(F32).T
        hole = holes[:, columns].astype(F32)
        hole = jnp.concatenate([hole, jnp.zeros((T - occ_rows, 2 * T), F32)], axis=0)
        hole = jnp.concatenate([hole, hole], axis=0).T
        for part in range(4):
            at = pl.ds((part % 2) * T + chunk * 2 + part // 2, H, stride=2 * T)
            spread_a[at, :] = turned[part * H : (part + 1) * H, : 2 * T]
            spread_b[at, :] = turned[part * H : (part + 1) * H, 2 * T :]
        for w in range(2):
            third = chunk * 2 + w
            at = lax.rem(third, H) * 2 * T + (third // H) * T
            holes_out[pl.ds(pl.multiple_of(at, T), T), :] = hole[w * T : (w + 1) * T].astype(BF16)
        return 0

    lax.fori_loop(0, H, one_chunk, 0, unroll=2)

    def settle(step, _):
        rows = pl.ds(pl.multiple_of(step * 2 * T, 2 * T), 2 * T)
        panels_out[rows, : 2 * T] = spread_a[rows, :].astype(BF16)
        panels_out[rows, 2 * T :] = spread_b[rows, :].astype(BF16)
        return 0

    lax.fori_loop(0, H, settle, 0, unroll=2)


def panels_of(integrals, holes):
    vmem = pl.BlockSpec(memory_space=pltpu.VMEM)
    return pl.pallas_call(
        panels_kernel,
        out_shape=(
            jax.ShapeDtypeStruct((T * T, 4 * T), BF16),
            jax.ShapeDtypeStruct((T * T, 2 * T), BF16),
        ),
        in_specs=[vmem, vmem],
        out_specs=[vmem, vmem],
        scratch_shapes=[pltpu.VMEM((T * T, 2 * T), F32)] * 2,
        compiler_params=pltpu.CompilerParams(vmem_limit_bytes=VMEM_LIMIT),
        cost_estimate=pl.CostEstimate(flops=1 << 28, bytes_accessed=5 << 20, transcendentals=0),
        name="panels",
    )(integrals, holes)


def terms_kernel(rel, triples, got_one, got_two, in1, in2, in3, panels, holes, out, chosen):
    virt = lax.axis_index("virt")
    y, core = virt // 2, lax.rem(virt, 2)
    off_i, off_j, live = row_of(triples, lax.axis_index("trip"), core, rel)
    which = jnp.where(live, off_i + off_j - 3, 3)
    for at, option in enumerate((got_one.at[0], got_one.at[1], got_two)):

        @pl.when(which == at)
        def _():
            chosen[...] = option[...]

    @pl.when(which == 3)
    def _():
        chosen[...] = jnp.zeros_like(chosen)

    blocks = (chosen, in1.at[rel], in2.at[rel], in3.at[rel])
    amps_lead, amps_dup, coul_lead, coul_dup = [], [], [], []
    for d in range(4):
        block = blocks[d][...]
        second = block[T : 2 * T]
        amps_lead.append(block[:T])
        amps_dup += [second, second]
        packed = block[2 * T :]
        coulomb = jnp.concatenate(
            [packed[:, g * T : (g + 1) * T] for g in range(4)], axis=0
        )
        coul_lead.append(coulomb)
        coul_dup += [coulomb, coulomb]
    amps_lead = jnp.concatenate(amps_lead, axis=0)
    amps_dup = jnp.concatenate(amps_dup, axis=0)
    coul_lead = jnp.concatenate(coul_lead, axis=0)
    coul_dup = jnp.concatenate(coul_dup, axis=0)
    low = lane_low(T)
    contract = (((1,), (1,)), ((), ()))

    def group(step, _):
        rows = pl.ds(pl.multiple_of(step * 8 * T, 8 * T), 8 * T)
        panel = panels[rows, :]
        hole = holes[rows, :T]
        by_rows = lax.dot_general(panel, amps_dup, contract, preferred_element_type=F32)
        by_rows += lax.dot_general(hole, coul_dup, contract, preferred_element_type=F32)
        by_cols = lax.dot_general(amps_lead, panel, contract, preferred_element_type=F32)
        by_cols += lax.dot_general(coul_lead, hole, contract, preferred_element_type=F32)
        own = lax.rem(step // 2 - y + 4, 4)
        for pair in range(4):
            row = pair * 2 * T
            for d in range(4):
                col = d * 2 * T
                tile = jnp.where(
                    low,
                    by_rows[row : row + T, col : col + 2 * T],
                    by_rows[row + T : row + 2 * T, col : col + 2 * T],
                )
                tile += by_cols[d * T : (d + 1) * T, row : row + 2 * T]
                if d == 0:
                    at = pl.multiple_of((lax.rem(step, 2) * 4 + pair) * T, T)
                    out[own, 0, pl.ds(at, T), :] = tile.astype(BF16)
                else:
                    at = pl.multiple_of((step * 4 + pair) * 16, 16)
                    for quarter in range(4):
                        rows16 = jnp.concatenate(
                            [
                                tile[8 * quarter : 8 * quarter + 8],
                                tile[H + 8 * quarter : H + 8 * quarter + 8],
                            ],
                            axis=0,
                        )
                        out[lax.rem(quarter - y + 4, 4), d, pl.ds(at, 16), :] = rows16.astype(BF16)
        return 0

    lax.fori_loop(0, 8, group, 0)


def terms(rel, triples, blocks, panels, holes):
    vmem = pl.BlockSpec(memory_space=pltpu.VMEM)
    return pl.pallas_call(
        functools.partial(terms_kernel, rel),
        out_shape=jax.ShapeDtypeStruct((4, 4, 512, 2 * T), BF16),
        in_specs=[pl.BlockSpec(memory_space=pltpu.SMEM)] + [vmem] * 7,
        out_specs=vmem,
        scratch_shapes=[pltpu.VMEM((BLOCK_ROWS, 4 * T), BF16)],
        compiler_params=pltpu.CompilerParams(vmem_limit_bytes=VMEM_LIMIT),
        cost_estimate=pl.CostEstimate(
            flops=2 * 4096 * 320 * 768, bytes_accessed=5 << 20, transcendentals=0
        ),
        name="terms",
    )(triples, *blocks, panels, holes)


def combine_kernel(triples, own, one, two, three, out, scratch):
    core = lax.rem(lax.axis_index("virt"), 2)
    _, off_j, _ = row_of(triples, lax.axis_index("trip"), core, 0)
    for index, part in enumerate((one, two, three)):
        scratch[index * 512 : (index + 1) * 512, :] = part[...].astype(F32)
    mid_is_j = jnp.full((T, 2 * T), off_j, jnp.int32) == 2

    def as_rows(index, cp):
        low_rows = scratch[pl.ds(index * 512 + cp, H, stride=16), :]
        high_rows = scratch[pl.ds(index * 512 + 8 + cp, H, stride=16), :]
        low = lane_low(H)
        top = jnp.where(low, low_rows, swap_halves(high_rows))
        bottom = jnp.where(low, swap_halves(low_rows), high_rows)
        return jnp.concatenate([top, bottom], axis=0)

    def turned(x):
        flat = x.T
        return jnp.concatenate([flat[:T], flat[T:]], axis=1)

    for cp in range(8):
        total = own[cp * T : (cp + 1) * T, :].astype(F32)
        total += as_rows(0, cp)
        middle = as_rows(1, cp)
        total += jnp.where(mid_is_j, middle, turned(middle))
        total += turned(as_rows(2, cp))
        out[cp * T : (cp + 1) * T, :] = total.astype(BF16)


def combine(triples, own, one, two, three):
    vmem = pl.BlockSpec(memory_space=pltpu.VMEM)
    return pl.pallas_call(
        combine_kernel,
        out_shape=jax.ShapeDtypeStruct((512, 2 * T), BF16),
        in_specs=[pl.BlockSpec(memory_space=pltpu.SMEM)] + [vmem] * 4,
        out_specs=vmem,
        scratch_shapes=[pltpu.VMEM((3 * 512, 2 * T), F32)],
        compiler_params=pltpu.CompilerParams(vmem_limit_bytes=VMEM_LIMIT),
        name="combine",
    )(triples, own, one, two, three)


def energy_kernel(triples, w0, w1, w2, w3, extra_a, extra_b, inverse, out, whole, flipped, acc, rows_b):
    virt = lax.axis_index("virt")
    y, core = virt // 2, lax.rem(virt, 2)
    _, _, live = row_of(triples, lax.axis_index("trip"), core, 0)
    for j, part in enumerate((w0, w1, w2, w3)):
        at = pl.multiple_of(lax.rem(y - j + 4, 4) * 512, 512)
        whole[pl.ds(at, 512), :] = part[...].astype(F32)

    def flip(b, _):
        across = whole[pl.ds(b, H, stride=T), :].T
        flipped[pl.ds(pl.multiple_of(b * H, H), H), :] = jnp.concatenate(
            [across[0:H], across[T : T + H], across[H:T], across[T + H :]], axis=1
        )
        return 0

    lax.fori_loop(0, T, flip, 0, unroll=4)
    acc[...] = jnp.zeros_like(acc)

    def pair(bp, _):
        from_flipped = pack_rows(flipped[pl.ds(bp, T, stride=H), :])
        from_whole = pack_rows(whole[pl.ds(pl.multiple_of(bp * T, T), T), :])
        for half in range(2):
            b = bp + H * half
            at = pl.ds(pl.multiple_of(b * H, H), H)
            plain = whole[pl.ds(b, H, stride=T), :]
            turned = flipped[at, :]
            inv = inverse[at, :]
            first = (4.0 * plain + from_flipped[half]) * (plain - turned + extra_a[at, :]) * inv
            second = plain * (from_flipped[half] - from_whole[half] + extra_b[at, :]) * inv
            acc[...] += first
            rows_b[pl.ds(b, 1), :] = jnp.sum(second, axis=0, keepdims=True)
        return 0

    lax.fori_loop(0, H, pair, 0, unroll=2)
    by_a = jnp.sum(acc[...], axis=0, keepdims=True)
    by_a = by_a[:, :T] + by_a[:, T:]
    by_b = jnp.sum(rows_b[...].T, axis=0, keepdims=True)
    out[...] = jnp.where(live, by_a + by_b, 0.0)


def energy_of(triples, parts, extra_a, extra_b, inverse):
    vmem = pl.BlockSpec(memory_space=pltpu.VMEM)
    return pl.pallas_call(
        energy_kernel,
        out_shape=jax.ShapeDtypeStruct((1, T), F32),
        in_specs=[pl.BlockSpec(memory_space=pltpu.SMEM)] + [vmem] * 7,
        out_specs=vmem,
        scratch_shapes=[
            pltpu.VMEM((H * T, 2 * T), F32),
            pltpu.VMEM((H * T, 2 * T), F32),
            pltpu.VMEM((H, 2 * T), F32),
            pltpu.VMEM((T, 2 * T), F32),
        ],
        compiler_params=pltpu.CompilerParams(vmem_limit_bytes=VMEM_LIMIT),
        name="energy",
    )(triples, *parts, extra_a, extra_b, inverse)


def tables_kernel(
    triples, own, one, two, three, virt_energy, extra_a, extra_b, inverse, columns, rows, scalars
):
    core = lax.rem(lax.axis_index("virt"), 2)
    off_i, off_j, _ = row_of(triples, lax.axis_index("trip"), core, 0)
    low = lane_low(H)

    def exch(table, index):
        return table[index * T : (index + 1) * T, :].astype(F32)

    def pick(options, index):
        result = options[-1]
        for at in range(len(options) - 1):
            result = jnp.where(index == at, options[at], result)
        return result

    kj = pick([exch(own, 0), exch(own, 1)], off_j - 1)
    ki = pick([exch(own, 1), exch(own, 2)], off_i - 2)
    ji = pick([exch(one, 0), exch(one, 1), exch(two, 0)], off_i + off_j - 3)
    kj_t, ki_t, ji_t = kj.T, ki.T, ji.T
    heads = [x[3 * T : 3 * T + 8, :].astype(F32) for x in (own, one, two, three)]
    head_i = pick([heads[2], heads[3]], off_i - 2)
    head_j = pick([heads[1], heads[2]], off_j - 1)
    head_k = heads[0]
    occ = head_i[1:2] + head_j[1:2] + head_k[1:2]
    occ = jnp.concatenate([occ, occ], axis=1)

    def dup(m):
        return jnp.concatenate([m, m], axis=1)

    def by_row(v):
        return jnp.broadcast_to(v, (2 * T, T)).T

    def by_c(column):
        return jnp.where(low, column[:H], column[H:])

    def packed(m):
        return jnp.concatenate([m[:H], m[H:]], axis=1)

    s_i, s_j, s_k, e_v = head_i[0:1], head_j[0:1], head_k[0:1], virt_energy[...]
    for at, v in enumerate((s_i, s_j, s_k, e_v)):
        scalars[at * T : (at + 1) * T, :] = by_row(v)
    si_a, sk_a, e_a = dup(s_i), dup(s_k), dup(e_v)
    si_c, sj_c, sk_c, e_c = (by_c(scalars[at * T : (at + 1) * T, :]) for at in range(4))
    for at, m in enumerate((kj, ji_t, kj_t, ji)):
        columns[at * H : (at + 1) * H, :] = packed(m).astype(BF16)
    for at, m in enumerate((kj_t, ji, ki_t - ki)):
        rows[at * T : (at + 1) * T, :] = dup(m)
    ki_diff = packed(ki - ki_t)
    kj_ac = packed(kj_t)
    ji_ca = packed(ji)
    base = occ - e_a - e_c
    source = lax.broadcasted_iota(jnp.int32, (2 * T, 2 * T), 0)
    target = lax.broadcasted_iota(jnp.int32, (2 * T, 2 * T), 1)
    same_half = (source >= T) == (target >= T)

    def one_b(b, _):
        at = pl.ds(pl.multiple_of(b * H, H), H)
        spread = jnp.where(same_half & (jnp.bitwise_and(source, T - 1) == b), 1.0, 0.0).astype(BF16)
        over_c = jnp.dot(columns[...], spread, preferred_element_type=F32)
        kj_cb, ji_bc, kj_bc, ji_cb = (over_c[g * H : (g + 1) * H] for g in range(4))
        kj_ab, ji_ba, ki_ab = (rows[pl.ds(g * T + b, 1), :] for g in range(3))
        si_b, sj_b, sk_b, e_b = (scalars[pl.ds(g * T + b, 1), :] for g in range(4))
        extra_a[at, :] = (
            si_a * kj_cb - si_c * kj_ab + sj_b * ki_diff + sk_c * ji_ba - sk_a * ji_bc
        )
        extra_b[at, :] = (
            si_b * kj_ac - si_a * kj_bc + sj_c * ki_ab + sk_a * ji_cb - sk_b * ji_ca
        )
        inverse[at, :] = 1.0 / (base - e_b)
        return 0

    lax.fori_loop(0, T, one_b, 0, unroll=2)


def tables(triples, small, virt_energy):
    vmem = pl.BlockSpec(memory_space=pltpu.VMEM)
    table = jax.ShapeDtypeStruct((H * T, 2 * T), F32)
    return pl.pallas_call(
        tables_kernel,
        out_shape=(table, table, table),
        in_specs=[pl.BlockSpec(memory_space=pltpu.SMEM)] + [vmem] * 5,
        out_specs=[vmem] * 3,
        scratch_shapes=[
            pltpu.VMEM((4 * H, 2 * T), BF16),
            pltpu.VMEM((3 * T, 2 * T), F32),
            pltpu.VMEM((4 * T, 2 * T), F32),
        ],
        compiler_params=pltpu.CompilerParams(vmem_limit_bytes=VMEM_LIMIT),
        cost_estimate=pl.CostEstimate(flops=1 << 28, bytes_accessed=3 << 20, transcendentals=0),
        name="tables",
    )(triples, *small, virt_energy)


def local(
    virt_integrals,
    pair_amps,
    hole_amps,
    coulomb_ints,
    exchange_ints,
    singles,
    occ_energy,
    virt_energy,
    triples,
):
    n_trip = lax.axis_size("trip")

    out1, out2, out3, up1, up2 = prep(
        triples, pair_amps.reshape(3, 2 * T, 4 * T), coulomb_ints.reshape(coulomb_ints.shape[1:])
    )
    got_two = lax.ppermute(up2, "trip", shift_route(n_trip, -2))
    in2 = lax.ppermute(out2, "trip", shift_route(n_trip, 2))
    got_one = lax.ppermute(up1, "trip", shift_route(n_trip, -1))
    in1 = lax.ppermute(out1, "trip", shift_route(n_trip, 1))
    in3 = lax.ppermute(out3, "trip", shift_route(n_trip, 3))
    blocks = (got_one, got_two, in1, in2, in3)

    panels, holes = panels_of(
        virt_integrals.reshape(4 * T, T * T), hole_amps.reshape(hole_amps.shape[1:])
    )

    send = terms(1, triples, blocks, panels, holes)
    got = lax.ppermute(send, "virt", CORE_ROUTE)
    keep = terms(0, triples, blocks, panels, holes)
    sums = [(keep[j].astype(F32) + got[j].astype(F32)) for j in range(4)]

    arrived = [lax.ppermute(sums[j].astype(BF16), "virt", ring_route(j)) for j in (1, 2, 3)]

    small = jnp.concatenate(
        [
            exchange_ints.reshape(3 * T, T),
            singles,
            jnp.broadcast_to(occ_energy[:, None], (1, T)),
            jnp.zeros((14, T), BF16),
        ],
        axis=0,
    )
    small, _ = lax.optimization_barrier((small, keep))
    smalls = [small] + [
        lax.ppermute(small, "trip", shift_route(n_trip, -d)) for d in (1, 2, 3)
    ]
    extra_a, extra_b, inverse = tables(triples, smalls, virt_energy.reshape(1, T))

    (extra_a, extra_b, inverse), arrived = lax.optimization_barrier(
        ((extra_a, extra_b, inverse), arrived)
    )
    total = sums[0] + arrived[0].astype(F32) + arrived[1].astype(F32) + arrived[2].astype(F32)
    shares = [
        lax.ppermute(total[d].astype(BF16), "trip", shift_route(n_trip, -d)) for d in (1, 2, 3)
    ]
    chunk = combine(triples, total[0], shares[0], shares[1], shares[2])
    parts = [chunk] + [lax.ppermute(chunk, "virt", ring_route(j)) for j in (1, 2, 3)]

    mine = energy_of(triples, parts, extra_a, extra_b, inverse)
    other = lax.ppermute(mine, "virt", CORE_ROUTE)
    first = lax.rem(lax.axis_index("virt"), 2) == 0
    return jnp.where(
        first, jnp.concatenate([mine, other], axis=0), jnp.concatenate([other, mine], axis=0)
    )


def solution(mesh):
    placed = (
        P("trip", "virt", None),
        P("trip", None, None, None, "virt"),
        P("trip", "virt", None),
        P("trip", None, "virt", None),
        P("trip", None, None),
        P("trip", None),
        P("trip"),
        P(),
        P("trip", None),
    )
    return jax.shard_map(
        local, mesh=mesh, in_specs=placed, out_specs=P("trip", None), check_vma=False
    )
```

```python
import functools

import jax
import jax.numpy as jnp
from jax import lax
from jax.experimental import pallas as pl
from jax.experimental.pallas import tpu as pltpu
from jax.sharding import PartitionSpec as P

T = 64
H = 32
F32 = jnp.float32
BF16 = jnp.bfloat16
CROWS = 16
BLOCK_ROWS = 2 * T + CROWS
SMALL_ROWS = 3 * H + 16
VMEM_LIMIT = 20 * 1024 * 1024


def shift_route(size, distance):
    return [(i, i + distance) for i in range(size) if 0 <= i + distance < size]


CORE_ROUTE = [(i, i ^ 1) for i in range(8)]


def lane_low(rows):
    return lax.broadcasted_iota(jnp.int32, (rows, 2 * T), 1) < T


def swap_halves(x):
    return pltpu.roll(x, T, 1)


def pack_rows(rows64):
    low = lane_low(H)
    top, bottom = rows64[:H], rows64[H:]
    first = jnp.where(low, top, swap_halves(bottom))
    second = jnp.where(low, swap_halves(top), bottom)
    return first, second


def row_of(triples, owner, core, rel):
    s = jnp.where(core == 0, rel, 1 - rel)
    live = triples[s, 0] >= 0
    off_i = jnp.where(live, triples[s, 0] - owner, 2)
    off_j = jnp.where(live, triples[s, 1] - owner, 1)
    return off_i, off_j, live


def prep_kernel(triples, amps_in, coulomb_in, out1, out2, out3, up1, up2, blocks, amps, coulomb, sems):
    copies = [
        pltpu.make_async_copy(amps_in, amps, sems.at[0]),
        pltpu.make_async_copy(coulomb_in, coulomb, sems.at[1]),
    ]
    for copy in copies:
        copy.start()
    for copy in copies:
        copy.wait()
    owner, core = lax.axis_index("trip"), lax.rem(lax.axis_index("virt"), 2)
    occ_rows = coulomb.shape[1]
    for s in range(3):
        blocks[s, : 2 * T, :] = amps[s]
        turned = jnp.concatenate(
            [coulomb[s].astype(F32), jnp.zeros((T - occ_rows, T), F32)], axis=0
        ).T
        packed = jnp.concatenate([-turned[g * CROWS : (g + 1) * CROWS] for g in range(4)], axis=1)
        blocks[s, 2 * T :, :] = packed.astype(BF16)
    up1[...] = blocks[0:2]
    up2[...] = blocks[0]
    for rel in range(2):
        off_i, off_j, live = row_of(triples, owner, core, rel)
        for d, out in ((1, out1), (2, out2), (3, out3)):
            takes_part = live & ((off_i == d) | (off_j == d))
            other = jnp.clip(off_i + off_j - d - 1, 0, 2)

            @pl.when(takes_part)
            def _():
                out[rel] = blocks[other]

            @pl.when(jnp.logical_not(takes_part))
            def _():
                out[rel] = jnp.zeros((BLOCK_ROWS, 4 * T), BF16)


def prep(triples, amps, coulomb):
    vmem = pl.BlockSpec(memory_space=pltpu.VMEM)
    two = jax.ShapeDtypeStruct((2, BLOCK_ROWS, 4 * T), BF16)
    one = jax.ShapeDtypeStruct((BLOCK_ROWS, 4 * T), BF16)
    return pl.pallas_call(
        prep_kernel,
        out_shape=(two, two, two, two, one),
        in_specs=[
            pl.BlockSpec(memory_space=pltpu.SMEM),
            pl.BlockSpec(memory_space=pltpu.HBM),
            pl.BlockSpec(memory_space=pltpu.HBM),
        ],
        out_specs=[vmem] * 5,
        scratch_shapes=[
            pltpu.VMEM((3, BLOCK_ROWS, 4 * T), BF16),
            pltpu.VMEM(amps.shape, BF16),
            pltpu.VMEM(coulomb.shape, BF16),
            pltpu.SemaphoreType.DMA((2,)),
        ],
        compiler_params=pltpu.CompilerParams(vmem_limit_bytes=VMEM_LIMIT),
        name="prep",
    )(triples, amps, coulomb)


STEPS = 8
DEPTH = 6 * T


def panels_kernel(integrals, holes, out, spread_a, spread_b):
    occ_rows = holes.shape[0]
    step = pl.program_id(0)
    per_step = H // STEPS

    for inner in range(per_step):
        chunk = step * per_step + inner
        columns = slice(inner * 2 * T, (inner + 1) * 2 * T)
        turned = integrals[:, columns].astype(F32).T
        hole = holes[:, columns].astype(F32)
        hole = jnp.concatenate([hole, jnp.zeros((2 * T - occ_rows, 2 * T), F32)], axis=0).T
        for part in range(4):
            at = pl.ds((part % 2) * T + chunk * 2 + part // 2, H, stride=2 * T)
            spread_a[at, :] = turned[part * H : (part + 1) * H, : 2 * T]
            spread_b[at, :] = turned[part * H : (part + 1) * H, 2 * T :]
        for w in range(2):
            third = chunk * 2 + w
            at = lax.rem(third, H) * 2 * T + (third // H) * T
            rows = pl.ds(pl.multiple_of(at, T), T)
            out[rows, 4 * T :] = hole[w * T : (w + 1) * T].astype(BF16)

    @pl.when(step == STEPS - 1)
    def _():
        def settle(step, _):
            rows = pl.ds(pl.multiple_of(step * 2 * T, 2 * T), 2 * T)
            out[rows, : 2 * T] = spread_a[rows, :].astype(BF16)
            out[rows, 2 * T : 4 * T] = spread_b[rows, :].astype(BF16)
            return 0

        lax.fori_loop(0, H, settle, 0, unroll=2)


def panels_of(integrals, holes):
    vmem = pl.BlockSpec(memory_space=pltpu.VMEM)
    columns = T * T // STEPS
    return pl.pallas_call(
        panels_kernel,
        grid=(STEPS,),
        out_shape=jax.ShapeDtypeStruct((T * T, DEPTH), BF16),
        in_specs=[
            pl.BlockSpec((4 * T, columns), lambda step: (0, step)),
            pl.BlockSpec((holes.shape[0], columns), lambda step: (0, step)),
        ],
        out_specs=vmem,
        scratch_shapes=[pltpu.VMEM((T * T, 2 * T), F32)] * 2,
        compiler_params=pltpu.CompilerParams(vmem_limit_bytes=VMEM_LIMIT),
        cost_estimate=pl.CostEstimate(flops=1 << 28, bytes_accessed=5 << 20, transcendentals=0),
        name="panels",
    )(integrals, holes)


def terms_kernel(rel, triples, got_one, got_two, in1, in2, in3, panels, out, chosen):
    core = lax.rem(lax.axis_index("virt"), 2)
    off_i, off_j, live = row_of(triples, lax.axis_index("trip"), core, rel)
    which = jnp.where(live, off_i + off_j - 3, 3)
    for at, option in enumerate((got_one.at[0], got_one.at[1], got_two)):

        @pl.when(which == at)
        def _():
            chosen[...] = option[...]

    @pl.when(which == 3)
    def _():
        chosen[...] = jnp.zeros_like(chosen)

    blocks = (chosen, in1.at[rel], in2.at[rel], in3.at[rel])
    lead, second = [], []
    for d in range(4):
        block = blocks[d][...]
        packed = block[2 * T :]
        coulomb = jnp.concatenate(
            [packed[:, g * T : (g + 1) * T] for g in range(4)], axis=0
        )
        coulomb = jnp.concatenate([coulomb, jnp.zeros_like(coulomb)], axis=1)
        lead.append(jnp.concatenate([block[:T], coulomb], axis=1))
        second.append(jnp.concatenate([block[T : 2 * T], coulomb], axis=1))
    lead = jnp.concatenate(lead, axis=0)
    second = jnp.concatenate(second, axis=0)
    low = lane_low(T)
    contract = (((1,), (1,)), ((), ()))

    def group(step, _):
        panel = panels[pl.ds(pl.multiple_of(step * 8 * T, 8 * T), 8 * T), :]
        by_rows = lax.dot_general(panel, second, contract, preferred_element_type=F32)
        by_cols = lax.dot_general(lead, panel, contract, preferred_element_type=F32)

        def tiles_of(pair, duo):
            row = pair * 2 * T
            lanes = slice(duo * 2 * T, (duo + 1) * 2 * T)
            upper, lower = by_rows[row : row + T, lanes], by_rows[row + T : row + 2 * T, lanes]
            first = jnp.where(low, upper, swap_halves(lower))
            other = jnp.where(low, swap_halves(upper), lower)
            at = 2 * duo * T
            return (
                first + by_cols[at : at + T, row : row + 2 * T],
                other + by_cols[at + T : at + 2 * T, row : row + 2 * T],
            )

        for two in range(2):
            evens = tiles_of(2 * two, 0) + tiles_of(2 * two, 1)
            odds = tiles_of(2 * two + 1, 0) + tiles_of(2 * two + 1, 1)
            for d, (even, odd) in enumerate(zip(evens, odds)):
                if d == 0:
                    quarter = step // 2
                    at = pl.ds(pl.multiple_of((lax.rem(step, 2) * 2 + two) * T, T), T)
                    out[0, quarter * 4, at, :] = jnp.where(low, even, swap_halves(odd)).astype(BF16)
                    out[1, quarter, at, :] = jnp.where(low, swap_halves(even), odd).astype(BF16)
                else:
                    at = pl.ds(pl.multiple_of((step * 4 + 2 * two) * 8, 16), 16)
                    for quarter in range(4):
                        for half in range(2):
                            c = slice(half * H + quarter * 8, half * H + quarter * 8 + 8)
                            rows16 = jnp.concatenate([even[c], odd[c]], axis=0).astype(BF16)
                            index = quarter * 4 + d if half == 0 else d * 4 + quarter
                            out[half, index, at, :] = rows16
        return 0

    lax.fori_loop(0, 8, group, 0)


def terms(rel, triples, blocks, panels):
    vmem = pl.BlockSpec(memory_space=pltpu.VMEM)
    return pl.pallas_call(
        functools.partial(terms_kernel, rel),
        out_shape=jax.ShapeDtypeStruct((2, 16, 256, 2 * T), BF16),
        in_specs=[pl.BlockSpec(memory_space=pltpu.SMEM)] + [vmem] * 6,
        out_specs=vmem,
        scratch_shapes=[pltpu.VMEM((BLOCK_ROWS, 4 * T), BF16)],
        compiler_params=pltpu.CompilerParams(vmem_limit_bytes=VMEM_LIMIT),
        cost_estimate=pl.CostEstimate(flops=1 << 31, bytes_accessed=5 << 20, transcendentals=0),
        name="terms",
    )(triples, *blocks, panels)


def add_kernel(keep, got, first, *second):
    for half, outs in ((0, [first]), (1, second)):
        per_out = 16 // len(outs)
        for at, out in enumerate(outs):

            def one(index, _):
                source = at * per_out + index
                total = keep[half, source].astype(F32) + got[half, source].astype(F32)
                out[index] = total.astype(BF16)
                return 0

            lax.fori_loop(0, per_out, one, 0)


def add(keep, got):
    vmem = pl.BlockSpec(memory_space=pltpu.VMEM)
    first = jax.ShapeDtypeStruct((16, 256, 2 * T), BF16)
    second = jax.ShapeDtypeStruct((4, 256, 2 * T), BF16)
    return pl.pallas_call(
        add_kernel,
        out_shape=(first,) + (second,) * 4,
        in_specs=[vmem] * 2,
        out_specs=[vmem] * 5,
        compiler_params=pltpu.CompilerParams(vmem_limit_bytes=VMEM_LIMIT),
        name="add",
    )(keep, got)


def gather_terms(mid_is_j, one, two, three, by_j, by_i):
    middle = two.astype(F32)
    by_j[...] = one.astype(F32) + jnp.where(mid_is_j, middle, 0.0)
    by_i[...] = three.astype(F32) + jnp.where(mid_is_j, 0.0, middle)


def turned_sum(own, by_j, by_i, base, q):
    low = lane_low(H)

    def as_rows(table):
        even = table[pl.ds(base + 2 * q, H, stride=8), :]
        odd = table[pl.ds(base + 2 * q + 1, H, stride=8), :]
        top = jnp.where(low, even, swap_halves(odd))
        bottom = jnp.where(low, swap_halves(even), odd)
        return jnp.concatenate([top, bottom], axis=0)

    flat = as_rows(by_i).T
    return own + as_rows(by_j) + jnp.concatenate([flat[:T], flat[T:]], axis=1)


def middle_is_j(triples):
    core = lax.rem(lax.axis_index("virt"), 2)
    _, off_j, _ = row_of(triples, lax.axis_index("trip"), core, 0)
    return off_j == 2


def combine_kernel(triples, own, one, two, three, out, by_j, by_i):
    mid_is_j = middle_is_j(triples)
    for quarter in range(4):
        rows = pl.ds(quarter * 256, 256)
        gather_terms(
            mid_is_j, one[quarter], two[quarter], three[quarter], by_j.at[rows], by_i.at[rows]
        )
    for quarter in range(4):
        for q in range(4):
            at = slice(q * T, (q + 1) * T)
            total = turned_sum(own[quarter, at, :].astype(F32), by_j, by_i, quarter * 256, q)
            out[quarter, at, :] = total.astype(BF16)


def combine(triples, own, one, two, three):
    vmem = pl.BlockSpec(memory_space=pltpu.VMEM)
    return pl.pallas_call(
        combine_kernel,
        out_shape=jax.ShapeDtypeStruct((4, 256, 2 * T), BF16),
        in_specs=[pl.BlockSpec(memory_space=pltpu.SMEM)] + [vmem] * 4,
        out_specs=vmem,
        scratch_shapes=[pltpu.VMEM((1024, 2 * T), F32)] * 2,
        compiler_params=pltpu.CompilerParams(vmem_limit_bytes=VMEM_LIMIT),
        name="combine",
    )(triples, own, one, two, three)


def finish_kernel(triples, own, one, two, three, others, out, by_j, by_i):
    gather_terms(middle_is_j(triples), one[:256], two[:256], three[:256], by_j, by_i)
    for q in range(4):
        at = slice(q * T, (q + 1) * T)
        total = turned_sum(own[at, :], by_j, by_i, 0, q).astype(BF16)
        second = sum(others[source, at, :].astype(F32) for source in range(4)).astype(BF16)
        for copy in range(4):
            out[copy, at, :] = total
            out[copy, 256 + q * T : 256 + (q + 1) * T, :] = second


def finish(triples, own, shares, others):
    vmem = pl.BlockSpec(memory_space=pltpu.VMEM)
    return pl.pallas_call(
        finish_kernel,
        out_shape=jax.ShapeDtypeStruct((4, 512, 2 * T), BF16),
        in_specs=[pl.BlockSpec(memory_space=pltpu.SMEM)] + [vmem] * 5,
        out_specs=vmem,
        scratch_shapes=[pltpu.VMEM((256, 2 * T), F32)] * 2,
        compiler_params=pltpu.CompilerParams(vmem_limit_bytes=VMEM_LIMIT),
        name="finish",
    )(triples, own, *shares, others)


def energy_kernel(triples, parts, extra_a, extra_b, inverse, out, whole, flipped, acc, rows_b):
    core = lax.rem(lax.axis_index("virt"), 2)
    _, _, live = row_of(triples, lax.axis_index("trip"), core, 0)
    low = lane_low(T)
    for quarter in range(4):
        for q in range(4):
            first = parts[quarter, q * T : (q + 1) * T, :].astype(F32)
            second = parts[quarter, 256 + q * T : 256 + (q + 1) * T, :].astype(F32)
            at = (quarter * 8 + 2 * q) * T
            whole[at : at + T, :] = jnp.where(low, first, swap_halves(second))
            whole[at + T : at + 2 * T, :] = jnp.where(low, swap_halves(first), second)

    low32 = lax.broadcasted_iota(jnp.int32, (H, 2 * T), 1) % T < H
    low_half = lane_low(H)

    def flip(step, _):
        b = step * 4
        across = jnp.concatenate(
            [whole[pl.ds(b + at, H, stride=T), :] for at in range(4)], axis=0
        ).T
        first = [across[at * H : (at + 1) * H] for at in (0, 2, 1, 3)]
        mid = [None] * 4
        for at in range(2):
            x, z = first[at], first[at + 2]
            mid[at] = jnp.where(low_half, x, swap_halves(z))
            mid[at + 2] = jnp.where(low_half, swap_halves(x), z)
        for at in (0, 2):
            x, z = mid[at], mid[at + 1]
            for inner, value in (
                (0, jnp.where(low32, x, pltpu.roll(z, H, 1))),
                (1, jnp.where(low32, pltpu.roll(x, 3 * H, 1), z)),
            ):
                rows = pl.ds(pl.multiple_of((b + at + inner) * H, H), H)
                flipped[rows, :] = value
        return 0

    lax.fori_loop(0, T // 4, flip, 0, unroll=2)
    acc[...] = jnp.zeros_like(acc)

    def pair(bp, _):
        from_flipped = pack_rows(flipped[pl.ds(bp, T, stride=H), :])
        from_whole = pack_rows(whole[pl.ds(pl.multiple_of(bp * T, T), T), :])
        for half in range(2):
            b = bp + H * half
            at = pl.ds(pl.multiple_of(b * H, H), H)
            plain = whole[pl.ds(b, H, stride=T), :]
            turned = flipped[at, :]
            inv = inverse[at, :]
            first = (4.0 * plain + from_flipped[half]) * (plain - turned + extra_a[at, :]) * inv
            second = plain * (from_flipped[half] - from_whole[half] + extra_b[at, :]) * inv
            acc[...] += first
            rows_b[pl.ds(b, 1), :] = jnp.sum(second, axis=0, keepdims=True)
        return 0

    lax.fori_loop(0, H, pair, 0, unroll=2)
    by_a = jnp.sum(acc[...], axis=0, keepdims=True)
    by_a = by_a[:, :T] + by_a[:, T:]
    by_b = jnp.sum(rows_b[...].T, axis=0, keepdims=True)
    out[...] = jnp.where(live, by_a + by_b, 0.0)


def energy_of(triples, parts, extra_a, extra_b, inverse):
    vmem = pl.BlockSpec(memory_space=pltpu.VMEM)
    return pl.pallas_call(
        energy_kernel,
        out_shape=jax.ShapeDtypeStruct((1, T), F32),
        in_specs=[pl.BlockSpec(memory_space=pltpu.SMEM)] + [vmem] * 4,
        out_specs=vmem,
        scratch_shapes=[
            pltpu.VMEM((H * T, 2 * T), F32),
            pltpu.VMEM((H * T, 2 * T), F32),
            pltpu.VMEM((H, 2 * T), F32),
            pltpu.VMEM((T, 2 * T), F32),
        ],
        compiler_params=pltpu.CompilerParams(vmem_limit_bytes=VMEM_LIMIT),
        name="energy",
    )(triples, parts, extra_a, extra_b, inverse)


def tables_kernel(
    triples, own, one, two, three, virt_energy, extra_a, extra_b, inverse, columns, rows, scalars
):
    core = lax.rem(lax.axis_index("virt"), 2)
    off_i, off_j, _ = row_of(triples, lax.axis_index("trip"), core, 0)
    low = lane_low(H)

    def small_of(table):
        return table[table.shape[0] - SMALL_ROWS :, :]

    def exch(table, index):
        flat = small_of(table)[index * H : (index + 1) * H, :].astype(F32)
        return jnp.concatenate([flat[:, :T], flat[:, T:]], axis=0)

    def pick(options, index):
        result = options[-1]
        for at in range(len(options) - 1):
            result = jnp.where(index == at, options[at], result)
        return result

    kj = pick([exch(own, 0), exch(own, 1)], off_j - 1)
    ki = pick([exch(own, 1), exch(own, 2)], off_i - 2)
    ji = pick([exch(one, 0), exch(one, 1), exch(two, 0)], off_i + off_j - 3)
    kj_t, ki_t, ji_t = kj.T, ki.T, ji.T
    heads = [small_of(x)[3 * H :, :].astype(F32) for x in (own, one, two, three)]
    head_i = pick([heads[2], heads[3]], off_i - 2)
    head_j = pick([heads[1], heads[2]], off_j - 1)
    head_k = heads[0]
    occ = head_i[0:1, T:] + head_j[0:1, T:] + head_k[0:1, T:]
    occ = jnp.concatenate([occ, occ], axis=1)

    def dup(m):
        return jnp.concatenate([m, m], axis=1)

    def by_row(v):
        return jnp.broadcast_to(v, (2 * T, T)).T

    def by_c(column):
        return jnp.where(low, column[:H], column[H:])

    def packed(m):
        return jnp.concatenate([m[:H], m[H:]], axis=1)

    s_i, s_j, s_k, e_v = (*(x[0:1, :T] for x in (head_i, head_j, head_k)), virt_energy[...])
    for at, v in enumerate((s_i, s_j, s_k, e_v)):
        scalars[at * T : (at + 1) * T, :] = by_row(v)
    si_a, sk_a, e_a = dup(s_i), dup(s_k), dup(e_v)
    si_c, sj_c, sk_c, e_c = (by_c(scalars[at * T : (at + 1) * T, :]) for at in range(4))
    for at, m in enumerate((kj, ji_t, kj_t, ji)):
        columns[at * H : (at + 1) * H, :] = packed(m).astype(BF16)
    for at, m in enumerate((kj_t, ji, ki_t - ki)):
        rows[at * T : (at + 1) * T, :] = dup(m)
    ki_diff = packed(ki - ki_t)
    kj_ac = packed(kj_t)
    ji_ca = packed(ji)
    base = occ - e_a - e_c
    source = lax.broadcasted_iota(jnp.int32, (2 * T, 2 * T), 0)
    target = lax.broadcasted_iota(jnp.int32, (2 * T, 2 * T), 1)
    same_half = (source >= T) == (target >= T)

    def one_b(b, _):
        at = pl.ds(pl.multiple_of(b * H, H), H)
        spread = jnp.where(same_half & (jnp.bitwise_and(source, T - 1) == b), 1.0, 0.0).astype(BF16)
        over_c = jnp.dot(columns[...], spread, preferred_element_type=F32)
        kj_cb, ji_bc, kj_bc, ji_cb = (over_c[g * H : (g + 1) * H] for g in range(4))
        kj_ab, ji_ba, ki_ab = (rows[pl.ds(g * T + b, 1), :] for g in range(3))
        si_b, sj_b, sk_b, e_b = (scalars[pl.ds(g * T + b, 1), :] for g in range(4))
        extra_a[at, :] = (
            si_a * kj_cb - si_c * kj_ab + sj_b * ki_diff + sk_c * ji_ba - sk_a * ji_bc
        )
        extra_b[at, :] = (
            si_b * kj_ac - si_a * kj_bc + sj_c * ki_ab + sk_a * ji_cb - sk_b * ji_ca
        )
        inverse[at, :] = 1.0 / (base - e_b)
        return 0

    lax.fori_loop(0, T, one_b, 0, unroll=2)


def tables(triples, small, virt_energy):
    vmem = pl.BlockSpec(memory_space=pltpu.VMEM)
    table = jax.ShapeDtypeStruct((H * T, 2 * T), F32)
    return pl.pallas_call(
        tables_kernel,
        out_shape=(table, table, table),
        in_specs=[pl.BlockSpec(memory_space=pltpu.SMEM)] + [vmem] * 5,
        out_specs=[vmem] * 3,
        scratch_shapes=[
            pltpu.VMEM((4 * H, 2 * T), BF16),
            pltpu.VMEM((3 * T, 2 * T), F32),
            pltpu.VMEM((4 * T, 2 * T), F32),
        ],
        compiler_params=pltpu.CompilerParams(vmem_limit_bytes=VMEM_LIMIT),
        cost_estimate=pl.CostEstimate(flops=1 << 28, bytes_accessed=3 << 20, transcendentals=0),
        name="tables",
    )(triples, *small, virt_energy)


def local(
    virt_integrals,
    pair_amps,
    hole_amps,
    coulomb_ints,
    exchange_ints,
    singles,
    occ_energy,
    virt_energy,
    triples,
):
    n_trip = lax.axis_size("trip")

    out1, out2, out3, up1, up2 = prep(
        triples, pair_amps.reshape(3, 2 * T, 4 * T), coulomb_ints.reshape(coulomb_ints.shape[1:])
    )
    got_two = lax.ppermute(up2, "trip", shift_route(n_trip, -2))
    in2 = lax.ppermute(out2, "trip", shift_route(n_trip, 2))
    got_one = lax.ppermute(up1, "trip", shift_route(n_trip, -1))
    in1 = lax.ppermute(out1, "trip", shift_route(n_trip, 1))
    in3 = lax.ppermute(out3, "trip", shift_route(n_trip, 3))
    blocks = (got_one, got_two, in1, in2, in3)

    panels = panels_of(
        virt_integrals.reshape(4 * T, T * T), hole_amps.reshape(hole_amps.shape[1:])
    )

    send = terms(1, triples, blocks, panels)
    got = lax.ppermute(send, "virt", CORE_ROUTE)
    keep = terms(0, triples, blocks, panels)
    first_half, *second_half = add(keep, got)
    over_y = functools.partial(
        lax.all_to_all,
        axis_name="virt",
        split_axis=0,
        concat_axis=0,
        axis_index_groups=[[0, 2, 4, 6], [1, 3, 5, 7]],
        tiled=True,
    )
    by_y = over_y(first_half)
    by_owner = [
        lax.ppermute(second_half[d], "trip", shift_route(n_trip, -d)) for d in (1, 2, 3)
    ]

    exchange = exchange_ints.reshape(3, 2, H, T)
    exchange = jnp.concatenate([exchange[:, 0], exchange[:, 1]], axis=2).reshape(3 * H, 2 * T)
    heads = jnp.concatenate([singles, jnp.broadcast_to(occ_energy[:, None], (1, T))], axis=1)
    small = jnp.concatenate([exchange, heads, jnp.zeros((15, 2 * T), BF16)], axis=0)
    total = by_y.reshape(4, 4, 256, 2 * T).astype(F32)
    total = total[0] + total[1] + total[2] + total[3]
    to_share = [jnp.concatenate([total[d].astype(BF16), small], axis=0) for d in (1, 2, 3)]
    shares = [
        lax.ppermute(to_share[d - 1], "trip", shift_route(n_trip, -d)) for d in (1, 2, 3)
    ]
    by_owner, _ = lax.optimization_barrier((by_owner, to_share))
    second_sums = over_y(combine(triples, second_half[0], *by_owner))

    chunk = finish(triples, total[0], shares, second_sums)
    parts = over_y(chunk)
    extra_a, extra_b, inverse = tables(triples, [small, *shares], virt_energy.reshape(1, T))

    mine = energy_of(triples, parts, extra_a, extra_b, inverse)
    other = lax.ppermute(mine, "virt", CORE_ROUTE)
    first = lax.rem(lax.axis_index("virt"), 2) == 0
    return jnp.where(
        first, jnp.concatenate([mine, other], axis=0), jnp.concatenate([other, mine], axis=0)
    )


def solution(mesh):
    placed = (
        P("trip", "virt", None),
        P("trip", None, None, None, "virt"),
        P("trip", "virt", None),
        P("trip", None, "virt", None),
        P("trip", None, None),
        P("trip", None),
        P("trip"),
        P(),
        P("trip", None),
    )
    return jax.shard_map(
        local, mesh=mesh, in_specs=placed, out_specs=P("trip", None), check_vma=False
    )
```

```python
import functools

import jax
import jax.numpy as jnp
from jax import lax
from jax.experimental import pallas as pl
from jax.experimental.pallas import tpu as pltpu
from jax.sharding import PartitionSpec as P

T = 64
H = 32
F32 = jnp.float32
BF16 = jnp.bfloat16
CROWS = 16
BLOCK_ROWS = 2 * T + CROWS
SMALL_ROWS = 3 * H + 16
VMEM_LIMIT = 20 * 1024 * 1024


def shift_route(size, distance):
    return [(i, i + distance) for i in range(size) if 0 <= i + distance < size]


CORE_ROUTE = [(i, i ^ 1) for i in range(8)]


def in_hbm(array):
    return pltpu.with_memory_space_constraint(array, pltpu.HBM)


def lane_low(rows):
    return lax.broadcasted_iota(jnp.int32, (rows, 2 * T), 1) < T


def swap_halves(x):
    return pltpu.roll(x, T, 1)


def pack_rows(rows64):
    low = lane_low(H)
    top, bottom = rows64[:H], rows64[H:]
    first = jnp.where(low, top, swap_halves(bottom))
    second = jnp.where(low, swap_halves(top), bottom)
    return first, second


def row_of(triples, owner, core, rel):
    s = jnp.where(core == 0, rel, 1 - rel)
    live = triples[s, 0] >= 0
    off_i = jnp.where(live, triples[s, 0] - owner, 2)
    off_j = jnp.where(live, triples[s, 1] - owner, 1)
    return off_i, off_j, live


def prep_kernel(triples, amps, coulomb, out1, out2, out3, up1, up2, blocks):
    owner, core = lax.axis_index("trip"), lax.rem(lax.axis_index("virt"), 2)
    occ_rows = coulomb.shape[1]
    for s in range(3):
        blocks[s, : 2 * T, :] = amps[s]
        turned = jnp.concatenate(
            [coulomb[s].astype(F32), jnp.zeros((T - occ_rows, T), F32)], axis=0
        ).T
        packed = jnp.concatenate([-turned[g * CROWS : (g + 1) * CROWS] for g in range(4)], axis=1)
        blocks[s, 2 * T :, :] = packed.astype(BF16)
    up1[...] = blocks[0:2]
    up2[...] = blocks[0]
    for rel in range(2):
        off_i, off_j, live = row_of(triples, owner, core, rel)
        for d, out in ((1, out1), (2, out2), (3, out3)):
            takes_part = live & ((off_i == d) | (off_j == d))
            other = jnp.clip(off_i + off_j - d - 1, 0, 2)

            @pl.when(takes_part)
            def _():
                out[rel] = blocks[other]

            @pl.when(jnp.logical_not(takes_part))
            def _():
                out[rel] = jnp.zeros((BLOCK_ROWS, 4 * T), BF16)


def prep(triples, amps, coulomb):
    vmem = pl.BlockSpec(memory_space=pltpu.VMEM)
    two = jax.ShapeDtypeStruct((2, BLOCK_ROWS, 4 * T), BF16)
    one = jax.ShapeDtypeStruct((BLOCK_ROWS, 4 * T), BF16)
    return pl.pallas_call(
        prep_kernel,
        out_shape=(two, two, two, two, one),
        in_specs=[pl.BlockSpec(memory_space=pltpu.SMEM), pl.BlockSpec(), pl.BlockSpec()],
        out_specs=[vmem] * 5,
        scratch_shapes=[
            pltpu.VMEM((3, BLOCK_ROWS, 4 * T), BF16),
        ],
        compiler_params=pltpu.CompilerParams(vmem_limit_bytes=VMEM_LIMIT),
        name="prep",
    )(triples, in_hbm(amps), in_hbm(coulomb))


STEPS = 8
DEPTH = 6 * T
PITCH = 2 * T + 8
WHOLE_PITCH = T + 8
FLIP_PITCH = H + 8


def panels_kernel(integrals_in, holes, out, spread_a, spread_b, integrals, sems):
    occ_rows = holes.shape[0]
    per_step = H // STEPS
    width = per_step * 2 * T
    copies = []
    for step in range(STEPS):
        span = pl.ds(step * width, width)
        copies.append(
            pltpu.make_async_copy(integrals_in.at[:, span], integrals.at[:, span], sems.at[step])
        )
    for copy in copies:
        copy.start()
    for step in range(STEPS):
        copies[step].wait()
        for chunk in range(step * per_step, (step + 1) * per_step):
            columns = slice(chunk * 2 * T, (chunk + 1) * 2 * T)
            turned = integrals[:, columns].astype(F32).T
            for part in range(4):
                at = pl.ds((part % 2) * T + chunk * 2 + part // 2, H, stride=PITCH)
                spread_a[at, :] = turned[part * H : (part + 1) * H, : 2 * T]
                spread_b[at, :] = turned[part * H : (part + 1) * H, 2 * T :]
    for chunk in range(H):
        hole = holes[:, chunk * 2 * T : (chunk + 1) * 2 * T].astype(F32)
        hole = jnp.concatenate([hole, jnp.zeros((2 * T - occ_rows, 2 * T), F32)], axis=0).T
        for w in range(2):
            third = chunk * 2 + w
            at = third % H * 2 * T + third // H * T
            out[at : at + T, 4 * T :] = hole[w * T : (w + 1) * T].astype(BF16)

    def settle(step, _):
        rows = pl.ds(pl.multiple_of(step * 2 * T, 2 * T), 2 * T)
        source = pl.ds(pl.multiple_of(step * PITCH, 8), 2 * T)
        out[rows, : 2 * T] = spread_a[source, :].astype(BF16)
        out[rows, 2 * T : 4 * T] = spread_b[source, :].astype(BF16)
        return 0

    lax.fori_loop(0, H, settle, 0, unroll=32)


def panels_of(integrals, holes):
    return pl.pallas_call(
        panels_kernel,
        out_shape=jax.ShapeDtypeStruct((T * T, DEPTH), BF16),
        in_specs=[pl.BlockSpec(memory_space=pltpu.HBM), pl.BlockSpec()],
        out_specs=pl.BlockSpec(memory_space=pltpu.VMEM),
        scratch_shapes=[pltpu.VMEM((H * PITCH, 2 * T), F32)] * 2
        + [
            pltpu.VMEM(integrals.shape, BF16),
            pltpu.SemaphoreType.DMA((STEPS,)),
        ],
        compiler_params=pltpu.CompilerParams(vmem_limit_bytes=VMEM_LIMIT),
        cost_estimate=pl.CostEstimate(flops=1 << 28, bytes_accessed=5 << 20, transcendentals=0),
        name="panels",
    )(in_hbm(integrals), in_hbm(holes))


def terms_kernel(rel, triples, got_one, got_two, in1, in2, in3, panels, out, chosen):
    core = lax.rem(lax.axis_index("virt"), 2)
    off_i, off_j, live = row_of(triples, lax.axis_index("trip"), core, rel)
    which = jnp.where(live, off_i + off_j - 3, 3)
    for at, option in enumerate((got_one.at[0], got_one.at[1], got_two)):

        @pl.when(which == at)
        def _():
            chosen[...] = option[...]

    @pl.when(which == 3)
    def _():
        chosen[...] = jnp.zeros_like(chosen)

    blocks = (chosen, in1.at[rel], in2.at[rel], in3.at[rel])
    lead, second = [], []
    for d in range(4):
        block = blocks[d][...]
        packed = block[2 * T :]
        coulomb = jnp.concatenate(
            [packed[:, g * T : (g + 1) * T] for g in range(4)], axis=0
        )
        coulomb = jnp.concatenate([coulomb, jnp.zeros_like(coulomb)], axis=1)
        lead.append(jnp.concatenate([block[:T], coulomb], axis=1))
        second.append(jnp.concatenate([block[T : 2 * T], coulomb], axis=1))
    lead = jnp.concatenate(lead, axis=0)
    second = jnp.concatenate(second, axis=0).astype(F32).T.astype(BF16)
    low = lane_low(T)
    contract = (((1,), (1,)), ((), ()))

    def group(step, _):
        panel = panels[pl.ds(pl.multiple_of(step * 8 * T, 8 * T), 8 * T), :]
        by_rows = jnp.dot(panel, second, preferred_element_type=F32)
        by_cols = lax.dot_general(lead, panel, contract, preferred_element_type=F32)

        def tiles_of(pair, duo):
            row = pair * 2 * T
            lanes = slice(duo * 2 * T, (duo + 1) * 2 * T)
            upper, lower = by_rows[row : row + T, lanes], by_rows[row + T : row + 2 * T, lanes]
            first = jnp.where(low, upper, swap_halves(lower))
            other = jnp.where(low, swap_halves(upper), lower)
            at = 2 * duo * T
            return (
                first + by_cols[at : at + T, row : row + 2 * T],
                other + by_cols[at + T : at + 2 * T, row : row + 2 * T],
            )

        for two in range(2):
            evens = tiles_of(2 * two, 0) + tiles_of(2 * two, 1)
            odds = tiles_of(2 * two + 1, 0) + tiles_of(2 * two + 1, 1)
            for d, (even, odd) in enumerate(zip(evens, odds)):
                if d == 0:
                    quarter = step // 2
                    at = pl.ds(pl.multiple_of((lax.rem(step, 2) * 2 + two) * T, T), T)
                    out[0, quarter * 4, at, :] = jnp.where(low, even, swap_halves(odd)).astype(BF16)
                    out[1, quarter, at, :] = jnp.where(low, swap_halves(even), odd).astype(BF16)
                else:
                    at = pl.ds(pl.multiple_of((step * 4 + 2 * two) * 8, 16), 16)
                    for quarter in range(4):
                        for half in range(2):
                            c = slice(half * H + quarter * 8, half * H + quarter * 8 + 8)
                            rows16 = jnp.concatenate([even[c], odd[c]], axis=0).astype(BF16)
                            index = quarter * 4 + d if half == 0 else d * 4 + quarter
                            out[half, index, at, :] = rows16
        return 0

    lax.fori_loop(0, 8, group, 0, unroll=8)


def terms(rel, triples, blocks, panels):
    vmem = pl.BlockSpec(memory_space=pltpu.VMEM)
    return pl.pallas_call(
        functools.partial(terms_kernel, rel),
        out_shape=jax.ShapeDtypeStruct((2, 16, 256, 2 * T), BF16),
        in_specs=[pl.BlockSpec(memory_space=pltpu.SMEM)] + [vmem] * 6,
        out_specs=vmem,
        scratch_shapes=[pltpu.VMEM((BLOCK_ROWS, 4 * T), BF16)],
        compiler_params=pltpu.CompilerParams(vmem_limit_bytes=VMEM_LIMIT),
        cost_estimate=pl.CostEstimate(flops=1 << 31, bytes_accessed=5 << 20, transcendentals=0),
        name="terms",
    )(triples, *blocks, panels)


def add_kernel(keep, got, first, *second):
    for half, outs in ((0, [first]), (1, second)):
        per_out = 16 // len(outs)
        for at, out in enumerate(outs):

            def one(index, _):
                source = at * per_out + index
                total = keep[half, source].astype(F32) + got[half, source].astype(F32)
                out[index] = total.astype(BF16)
                return 0

            lax.fori_loop(0, per_out, one, 0, unroll=4)


def add(keep, got):
    vmem = pl.BlockSpec(memory_space=pltpu.VMEM)
    first = jax.ShapeDtypeStruct((16, 256, 2 * T), BF16)
    second = jax.ShapeDtypeStruct((4, 256, 2 * T), BF16)
    return pl.pallas_call(
        add_kernel,
        out_shape=(first,) + (second,) * 4,
        in_specs=[vmem] * 2,
        out_specs=[vmem] * 5,
        compiler_params=pltpu.CompilerParams(vmem_limit_bytes=VMEM_LIMIT),
        name="add",
    )(keep, got)


def gather_terms(mid_is_j, one, two, three, by_j, by_i):
    middle = two.astype(F32)
    by_j[...] = one.astype(F32) + jnp.where(mid_is_j, middle, 0.0)
    by_i[...] = three.astype(F32) + jnp.where(mid_is_j, 0.0, middle)


def turned_sum(own, by_j, by_i, base, q):
    low = lane_low(H)

    def as_rows(table):
        even = table[pl.ds(base + 2 * q, H, stride=8), :]
        odd = table[pl.ds(base + 2 * q + 1, H, stride=8), :]
        top = jnp.where(low, even, swap_halves(odd))
        bottom = jnp.where(low, swap_halves(even), odd)
        return jnp.concatenate([top, bottom], axis=0)

    flat = as_rows(by_i).T
    return own + as_rows(by_j) + jnp.concatenate([flat[:T], flat[T:]], axis=1)


def middle_is_j(triples):
    core = lax.rem(lax.axis_index("virt"), 2)
    _, off_j, _ = row_of(triples, lax.axis_index("trip"), core, 0)
    return off_j == 2


def combine_kernel(triples, own, one, two, three, out, by_j, by_i):
    mid_is_j = middle_is_j(triples)
    for quarter in range(4):
        rows = pl.ds(quarter * 256, 256)
        gather_terms(
            mid_is_j, one[quarter], two[quarter], three[quarter], by_j.at[rows], by_i.at[rows]
        )
    for quarter in range(4):
        for q in range(4):
            at = slice(q * T, (q + 1) * T)
            total = turned_sum(own[quarter, at, :].astype(F32), by_j, by_i, quarter * 256, q)
            out[quarter, at, :] = total.astype(BF16)


def combine(triples, own, one, two, three):
    vmem = pl.BlockSpec(memory_space=pltpu.VMEM)
    return pl.pallas_call(
        combine_kernel,
        out_shape=jax.ShapeDtypeStruct((4, 256, 2 * T), BF16),
        in_specs=[pl.BlockSpec(memory_space=pltpu.SMEM)] + [vmem] * 4,
        out_specs=vmem,
        scratch_shapes=[pltpu.VMEM((1024, 2 * T), F32)] * 2,
        compiler_params=pltpu.CompilerParams(vmem_limit_bytes=VMEM_LIMIT),
        name="combine",
    )(triples, own, one, two, three)


def finish_kernel(triples, own, one, two, three, others, out, by_j, by_i):
    gather_terms(middle_is_j(triples), one[:256], two[:256], three[:256], by_j, by_i)
    for q in range(4):
        at = slice(q * T, (q + 1) * T)
        total = turned_sum(own[at, :], by_j, by_i, 0, q).astype(BF16)
        second = sum(others[source, at, :].astype(F32) for source in range(4)).astype(BF16)
        for copy in range(4):
            out[copy, at, :] = total
            out[copy, 256 + q * T : 256 + (q + 1) * T, :] = second


def finish(triples, own, shares, others):
    vmem = pl.BlockSpec(memory_space=pltpu.VMEM)
    return pl.pallas_call(
        finish_kernel,
        out_shape=jax.ShapeDtypeStruct((4, 512, 2 * T), BF16),
        in_specs=[pl.BlockSpec(memory_space=pltpu.SMEM)] + [vmem] * 5,
        out_specs=vmem,
        scratch_shapes=[pltpu.VMEM((256, 2 * T), F32)] * 2,
        compiler_params=pltpu.CompilerParams(vmem_limit_bytes=VMEM_LIMIT),
        name="finish",
    )(triples, own, *shares, others)


def energy_kernel(triples, parts, extra_a, extra_b, inverse, out, whole, flipped, acc, rows_b):
    core = lax.rem(lax.axis_index("virt"), 2)
    _, _, live = row_of(triples, lax.axis_index("trip"), core, 0)
    low = lane_low(T)
    for quarter in range(4):
        for q in range(4):
            first = parts[quarter, q * T : (q + 1) * T, :].astype(F32)
            second = parts[quarter, 256 + q * T : 256 + (q + 1) * T, :].astype(F32)
            at = (quarter * 8 + 2 * q) * WHOLE_PITCH
            whole[at : at + T, :] = jnp.where(low, first, swap_halves(second))
            at += WHOLE_PITCH
            whole[at : at + T, :] = jnp.where(low, swap_halves(first), second)

    low32 = lax.broadcasted_iota(jnp.int32, (H, 2 * T), 1) % T < H
    low_half = lane_low(H)

    def flip(step, _):
        b = step * 4
        across = jnp.concatenate(
            [whole[pl.ds(b + at, H, stride=WHOLE_PITCH), :] for at in range(4)], axis=0
        ).T
        first = [across[at * H : (at + 1) * H] for at in (0, 2, 1, 3)]
        mid = [None] * 4
        for at in range(2):
            x, z = first[at], first[at + 2]
            mid[at] = jnp.where(low_half, x, swap_halves(z))
            mid[at + 2] = jnp.where(low_half, swap_halves(x), z)
        for at in (0, 2):
            x, z = mid[at], mid[at + 1]
            for inner, value in (
                (0, jnp.where(low32, x, pltpu.roll(z, H, 1))),
                (1, jnp.where(low32, pltpu.roll(x, 3 * H, 1), z)),
            ):
                rows = pl.ds(pl.multiple_of((b + at + inner) * FLIP_PITCH, 8), H)
                flipped[rows, :] = value
        return 0

    lax.fori_loop(0, T // 4, flip, 0, unroll=8)
    acc[...] = jnp.zeros_like(acc)

    def pair(bp, _):
        from_flipped = pack_rows(flipped[pl.ds(bp, T, stride=FLIP_PITCH), :])
        from_whole = pack_rows(whole[pl.ds(pl.multiple_of(bp * WHOLE_PITCH, 8), T), :])
        for half in range(2):
            b = bp + H * half
            at = pl.ds(pl.multiple_of(b * H, H), H)
            plain = whole[pl.ds(b, H, stride=WHOLE_PITCH), :]
            turned = flipped[pl.ds(pl.multiple_of(b * FLIP_PITCH, 8), H), :]
            inv = inverse[at, :]
            first = (4.0 * plain + from_flipped[half]) * (plain - turned + extra_a[at, :]) * inv
            second = plain * (from_flipped[half] - from_whole[half] + extra_b[at, :]) * inv
            acc[...] += first
            rows_b[pl.ds(b, 1), :] = jnp.sum(second, axis=0, keepdims=True)
        return 0

    lax.fori_loop(0, H, pair, 0, unroll=8)
    by_a = jnp.sum(acc[...], axis=0, keepdims=True)
    by_a = by_a[:, :T] + by_a[:, T:]
    by_b = jnp.sum(rows_b[...].T, axis=0, keepdims=True)
    out[...] = jnp.where(live, by_a + by_b, 0.0)


def energy_of(triples, parts, extra_a, extra_b, inverse):
    vmem = pl.BlockSpec(memory_space=pltpu.VMEM)
    return pl.pallas_call(
        energy_kernel,
        out_shape=jax.ShapeDtypeStruct((1, T), F32),
        in_specs=[pl.BlockSpec(memory_space=pltpu.SMEM)] + [vmem] * 4,
        out_specs=vmem,
        scratch_shapes=[
            pltpu.VMEM((H * WHOLE_PITCH, 2 * T), F32),
            pltpu.VMEM((T * FLIP_PITCH, 2 * T), F32),
            pltpu.VMEM((H, 2 * T), F32),
            pltpu.VMEM((T, 2 * T), F32),
        ],
        compiler_params=pltpu.CompilerParams(vmem_limit_bytes=VMEM_LIMIT),
        name="energy",
    )(triples, parts, extra_a, extra_b, inverse)


def tables_kernel(
    triples, own, one, two, three, virt_energy, extra_a, extra_b, inverse, columns, rows, scalars
):
    core = lax.rem(lax.axis_index("virt"), 2)
    off_i, off_j, _ = row_of(triples, lax.axis_index("trip"), core, 0)
    low = lane_low(H)

    def small_of(table):
        return table[table.shape[0] - SMALL_ROWS :, :]

    def exch(table, index):
        flat = small_of(table)[index * H : (index + 1) * H, :].astype(F32)
        return jnp.concatenate([flat[:, :T], flat[:, T:]], axis=0)

    def pick(options, index):
        result = options[-1]
        for at in range(len(options) - 1):
            result = jnp.where(index == at, options[at], result)
        return result

    kj = pick([exch(own, 0), exch(own, 1)], off_j - 1)
    ki = pick([exch(own, 1), exch(own, 2)], off_i - 2)
    ji = pick([exch(one, 0), exch(one, 1), exch(two, 0)], off_i + off_j - 3)
    kj_t, ki_t, ji_t = kj.T, ki.T, ji.T
    heads = [small_of(x)[3 * H :, :].astype(F32) for x in (own, one, two, three)]
    head_i = pick([heads[2], heads[3]], off_i - 2)
    head_j = pick([heads[1], heads[2]], off_j - 1)
    head_k = heads[0]
    occ = head_i[0:1, T:] + head_j[0:1, T:] + head_k[0:1, T:]
    occ = jnp.concatenate([occ, occ], axis=1)

    def dup(m):
        return jnp.concatenate([m, m], axis=1)

    def by_row(v):
        return jnp.broadcast_to(v, (2 * T, T)).T

    def by_c(column):
        return jnp.where(low, column[:H], column[H:])

    def packed(m):
        return jnp.concatenate([m[:H], m[H:]], axis=1)

    s_i, s_j, s_k, e_v = (*(x[0:1, :T] for x in (head_i, head_j, head_k)), virt_energy[...])
    for at, v in enumerate((s_i, s_j, s_k, e_v)):
        scalars[at * T : (at + 1) * T, :] = by_row(v)
    si_a, sk_a, e_a = dup(s_i), dup(s_k), dup(e_v)
    si_c, sj_c, sk_c, e_c = (by_c(scalars[at * T : (at + 1) * T, :]) for at in range(4))
    for at, m in enumerate((kj, ji_t, kj_t, ji)):
        columns[at * H : (at + 1) * H, :] = packed(m).astype(BF16)
    for at, m in enumerate((kj_t, ji, ki_t - ki)):
        rows[at * T : (at + 1) * T, :] = dup(m)
    ki_diff = packed(ki - ki_t)
    kj_ac = packed(kj_t)
    ji_ca = packed(ji)
    base = occ - e_a - e_c
    source = lax.broadcasted_iota(jnp.int32, (2 * T, 2 * T), 0)
    target = lax.broadcasted_iota(jnp.int32, (2 * T, 2 * T), 1)
    same_half = (source >= T) == (target >= T)

    def one_b(b, _):
        at = pl.ds(pl.multiple_of(b * H, H), H)
        spread = jnp.where(same_half & (jnp.bitwise_and(source, T - 1) == b), 1.0, 0.0).astype(BF16)
        over_c = jnp.dot(columns[...], spread, preferred_element_type=F32)
        kj_cb, ji_bc, kj_bc, ji_cb = (over_c[g * H : (g + 1) * H] for g in range(4))
        kj_ab, ji_ba, ki_ab = (rows[pl.ds(g * T + b, 1), :] for g in range(3))
        si_b, sj_b, sk_b, e_b = (scalars[pl.ds(g * T + b, 1), :] for g in range(4))
        extra_a[at, :] = (
            si_a * kj_cb - si_c * kj_ab + sj_b * ki_diff + sk_c * ji_ba - sk_a * ji_bc
        )
        extra_b[at, :] = (
            si_b * kj_ac - si_a * kj_bc + sj_c * ki_ab + sk_a * ji_cb - sk_b * ji_ca
        )
        inverse[at, :] = 1.0 / (base - e_b)
        return 0

    lax.fori_loop(0, T, one_b, 0, unroll=8)


def tables(triples, small, virt_energy):
    vmem = pl.BlockSpec(memory_space=pltpu.VMEM)
    table = jax.ShapeDtypeStruct((H * T, 2 * T), F32)
    return pl.pallas_call(
        tables_kernel,
        out_shape=(table, table, table),
        in_specs=[pl.BlockSpec(memory_space=pltpu.SMEM)] + [vmem] * 5,
        out_specs=[vmem] * 3,
        scratch_shapes=[
            pltpu.VMEM((4 * H, 2 * T), BF16),
            pltpu.VMEM((3 * T, 2 * T), F32),
            pltpu.VMEM((4 * T, 2 * T), F32),
        ],
        compiler_params=pltpu.CompilerParams(vmem_limit_bytes=VMEM_LIMIT),
        cost_estimate=pl.CostEstimate(flops=1 << 28, bytes_accessed=3 << 20, transcendentals=0),
        name="tables",
    )(triples, *small, virt_energy)


def local(
    virt_integrals,
    pair_amps,
    hole_amps,
    coulomb_ints,
    exchange_ints,
    singles,
    occ_energy,
    virt_energy,
    triples,
):
    n_trip = lax.axis_size("trip")

    out1, out2, out3, up1, up2 = prep(
        triples, pair_amps.reshape(3, 2 * T, 4 * T), coulomb_ints.reshape(coulomb_ints.shape[1:])
    )
    got_two = lax.ppermute(up2, "trip", shift_route(n_trip, -2))
    in2 = lax.ppermute(out2, "trip", shift_route(n_trip, 2))
    got_one = lax.ppermute(up1, "trip", shift_route(n_trip, -1))
    in1 = lax.ppermute(out1, "trip", shift_route(n_trip, 1))
    in3 = lax.ppermute(out3, "trip", shift_route(n_trip, 3))
    blocks = (got_one, got_two, in1, in2, in3)

    panels = panels_of(
        virt_integrals.reshape(4 * T, T * T), hole_amps.reshape(hole_amps.shape[1:])
    )

    send = terms(1, triples, blocks, panels)
    got = lax.ppermute(send, "virt", CORE_ROUTE)
    keep = terms(0, triples, blocks, panels)
    first_half, *second_half = add(keep, got)
    over_y = functools.partial(
        lax.all_to_all,
        axis_name="virt",
        split_axis=0,
        concat_axis=0,
        axis_index_groups=[[0, 2, 4, 6], [1, 3, 5, 7]],
        tiled=True,
    )
    by_y = over_y(first_half)
    by_owner = [
        lax.ppermute(second_half[d], "trip", shift_route(n_trip, -d)) for d in (1, 2, 3)
    ]

    exchange = exchange_ints.reshape(3, 2, H, T)
    exchange = jnp.concatenate([exchange[:, 0], exchange[:, 1]], axis=2).reshape(3 * H, 2 * T)
    heads = jnp.concatenate([singles, jnp.broadcast_to(occ_energy[:, None], (1, T))], axis=1)
    small = jnp.concatenate([exchange, heads, jnp.zeros((15, 2 * T), BF16)], axis=0)
    total = by_y.reshape(4, 4, 256, 2 * T).astype(F32)
    total = total[0] + total[1] + total[2] + total[3]
    to_share = [jnp.concatenate([total[d].astype(BF16), small], axis=0) for d in (1, 2, 3)]
    shares = [
        lax.ppermute(to_share[d - 1], "trip", shift_route(n_trip, -d)) for d in (1, 2, 3)
    ]
    by_owner, _ = lax.optimization_barrier((by_owner, to_share))
    second_sums = over_y(combine(triples, second_half[0], *by_owner))

    chunk = finish(triples, total[0], shares, second_sums)
    parts = over_y(chunk)
    extra_a, extra_b, inverse = tables(triples, [small, *shares], virt_energy.reshape(1, T))

    mine = energy_of(triples, parts, extra_a, extra_b, inverse)
    other = lax.ppermute(mine, "virt", CORE_ROUTE)
    first = lax.rem(lax.axis_index("virt"), 2) == 0
    return jnp.where(
        first, jnp.concatenate([mine, other], axis=0), jnp.concatenate([other, mine], axis=0)
    )


def solution(mesh):
    placed = (
        P("trip", "virt", None),
        P("trip", None, None, None, "virt"),
        P("trip", "virt", None),
        P("trip", None, "virt", None),
        P("trip", None, None),
        P("trip", None),
        P("trip"),
        P(),
        P("trip", None),
    )
    return jax.shard_map(
        local, mesh=mesh, in_specs=placed, out_specs=P("trip", None), check_vma=False
    )
```

```python
import functools

import jax
import jax.numpy as jnp
from jax import lax
from jax.experimental import pallas as pl
from jax.experimental.pallas import tpu as pltpu
from jax.sharding import PartitionSpec as P

T = 64
H = 32
F32 = jnp.float32
BF16 = jnp.bfloat16
CROWS = 16
BLOCK_ROWS = 2 * T + CROWS
SMALL_ROWS = 3 * H + 16
VMEM_LIMIT = 12 * 1024 * 1024


def shift_route(size, distance):
    return [(i, i + distance) for i in range(size) if 0 <= i + distance < size]


CORE_ROUTE = [(i, i ^ 1) for i in range(8)]


def in_hbm(array):
    return pltpu.with_memory_space_constraint(array, pltpu.HBM)


def lane_low(rows):
    return lax.broadcasted_iota(jnp.int32, (rows, 2 * T), 1) < T


def swap_halves(x):
    return pltpu.roll(x, T, 1)


def row_of(triples, owner, core, rel):
    s = jnp.where(core == 0, rel, 1 - rel)
    live = triples[s, 0] >= 0
    off_i = jnp.where(live, triples[s, 0] - owner, 2)
    off_j = jnp.where(live, triples[s, 1] - owner, 1)
    return off_i, off_j, live


def prep_kernel(triples, amps, coulomb, out1, out2, out3, up1, up2, blocks):
    owner, core = lax.axis_index("trip"), lax.rem(lax.axis_index("virt"), 2)
    occ_rows = coulomb.shape[1]
    for s in range(3):
        blocks[s, : 2 * T, :] = amps[s]
        turned = jnp.concatenate(
            [coulomb[s].astype(F32), jnp.zeros((T - occ_rows, T), F32)], axis=0
        ).T
        packed = jnp.concatenate([-turned[g * CROWS : (g + 1) * CROWS] for g in range(4)], axis=1)
        blocks[s, 2 * T :, :] = packed.astype(BF16)
    up1[...] = blocks[0:2]
    up2[...] = blocks[0]
    for rel in range(2):
        off_i, off_j, live = row_of(triples, owner, core, rel)
        for d, out in ((1, out1), (2, out2), (3, out3)):
            takes_part = live & ((off_i == d) | (off_j == d))
            other = jnp.clip(off_i + off_j - d - 1, 0, 2)

            @pl.when(takes_part)
            def _():
                out[rel] = blocks[other]

            @pl.when(jnp.logical_not(takes_part))
            def _():
                out[rel] = jnp.zeros((BLOCK_ROWS, 4 * T), BF16)


def prep(triples, amps, coulomb):
    vmem = pl.BlockSpec(memory_space=pltpu.VMEM)
    two = jax.ShapeDtypeStruct((2, BLOCK_ROWS, 4 * T), BF16)
    one = jax.ShapeDtypeStruct((BLOCK_ROWS, 4 * T), BF16)
    return pl.pallas_call(
        prep_kernel,
        out_shape=(two, two, two, two, one),
        in_specs=[pl.BlockSpec(memory_space=pltpu.SMEM), pl.BlockSpec(), pl.BlockSpec()],
        out_specs=[vmem] * 5,
        scratch_shapes=[
            pltpu.VMEM((3, BLOCK_ROWS, 4 * T), BF16),
        ],
        compiler_params=pltpu.CompilerParams(vmem_limit_bytes=VMEM_LIMIT),
        name="prep",
    )(triples, in_hbm(amps), in_hbm(coulomb))


STEPS = 8
DEPTH = 6 * T
PITCH = 2 * T + 8


def panels_kernel(integrals_in, holes, out, spread_a, spread_b, integrals, sems):
    occ_rows = holes.shape[0]
    per_step = H // STEPS
    width = per_step * 2 * T
    copies = []
    for step in range(STEPS):
        span = pl.ds(step * width, width)
        copies.append(
            pltpu.make_async_copy(integrals_in.at[:, span], integrals.at[:, span], sems.at[step])
        )
    for copy in copies:
        copy.start()
    for step in range(STEPS):
        copies[step].wait()
        for chunk in range(step * per_step, (step + 1) * per_step):
            columns = slice(chunk * 2 * T, (chunk + 1) * 2 * T)
            turned = integrals[:, columns].astype(F32).T
            for part in range(4):
                at = pl.ds((part % 2) * T + chunk * 2 + part // 2, H, stride=PITCH)
                spread_a[at, :] = turned[part * H : (part + 1) * H, : 2 * T]
                spread_b[at, :] = turned[part * H : (part + 1) * H, 2 * T :]
    for chunk in range(H):
        hole = holes[:, chunk * 2 * T : (chunk + 1) * 2 * T].astype(F32)
        hole = jnp.concatenate([hole, jnp.zeros((2 * T - occ_rows, 2 * T), F32)], axis=0).T
        for w in range(2):
            third = chunk * 2 + w
            at = third % H * 2 * T + third // H * T
            out[at : at + T, 4 * T :] = hole[w * T : (w + 1) * T].astype(BF16)

    def settle(step, _):
        rows = pl.ds(pl.multiple_of(step * 2 * T, 2 * T), 2 * T)
        source = pl.ds(pl.multiple_of(step * PITCH, 8), 2 * T)
        out[rows, : 2 * T] = spread_a[source, :].astype(BF16)
        out[rows, 2 * T : 4 * T] = spread_b[source, :].astype(BF16)
        return 0

    lax.fori_loop(0, H, settle, 0, unroll=32)


def panels_of(integrals, holes):
    return pl.pallas_call(
        panels_kernel,
        out_shape=jax.ShapeDtypeStruct((T * T, DEPTH), BF16),
        in_specs=[pl.BlockSpec(memory_space=pltpu.HBM), pl.BlockSpec()],
        out_specs=pl.BlockSpec(memory_space=pltpu.VMEM),
        scratch_shapes=[pltpu.VMEM((H * PITCH, 2 * T), F32)] * 2
        + [
            pltpu.VMEM(integrals.shape, BF16),
            pltpu.SemaphoreType.DMA((STEPS,)),
        ],
        compiler_params=pltpu.CompilerParams(vmem_limit_bytes=VMEM_LIMIT),
        cost_estimate=pl.CostEstimate(flops=1 << 28, bytes_accessed=5 << 20, transcendentals=0),
        name="panels",
    )(in_hbm(integrals), in_hbm(holes))


def terms_kernel(rel, triples, got_one, got_two, in1, in2, in3, panels, out, chosen):
    core = lax.rem(lax.axis_index("virt"), 2)
    off_i, off_j, live = row_of(triples, lax.axis_index("trip"), core, rel)
    which = jnp.where(live, off_i + off_j - 3, 3)
    for at, option in enumerate((got_one.at[0], got_one.at[1], got_two)):

        @pl.when(which == at)
        def _():
            chosen[...] = option[...]

    @pl.when(which == 3)
    def _():
        chosen[...] = jnp.zeros_like(chosen)

    blocks = (chosen, in1.at[rel], in2.at[rel], in3.at[rel])
    lead, second = [], []
    for d in range(4):
        block = blocks[d][...]
        packed = block[2 * T :]
        coulomb = jnp.concatenate(
            [packed[:, g * T : (g + 1) * T] for g in range(4)], axis=0
        )
        coulomb = jnp.concatenate([coulomb, jnp.zeros_like(coulomb)], axis=1)
        lead.append(jnp.concatenate([block[:T], coulomb], axis=1))
        second.append(jnp.concatenate([block[T : 2 * T], coulomb], axis=1))
    lead = jnp.concatenate(lead, axis=0)
    second = jnp.concatenate(second, axis=0).astype(F32).T.astype(BF16)
    low = lane_low(T)
    contract = (((1,), (1,)), ((), ()))

    eighth = lax.broadcasted_iota(jnp.int32, (8, 2 * T), 1) // 8
    odd_eighth = jnp.bitwise_and(eighth, 1) == 1
    high_eighth = jnp.bitwise_and(eighth, 2) == 2

    def skewed(tile):
        result = []
        for half in range(2):
            rows = [tile[half * H + 8 * at : half * H + 8 * at + 8] for at in range(4)]
            rows = [jnp.where(odd_eighth, rows[(j - 1) % 4], rows[j]) for j in range(4)]
            result.append([jnp.where(high_eighth, rows[(j - 2) % 4], rows[j]) for j in range(4)])
        return result

    def group(step, _):
        panel = panels[pl.ds(pl.multiple_of(step * 8 * T, 8 * T), 8 * T), :]
        by_rows = jnp.dot(panel, second, preferred_element_type=F32)
        by_cols = lax.dot_general(lead, panel, contract, preferred_element_type=F32)

        def tiles_of(pair, duo):
            row = pair * 2 * T
            lanes = slice(duo * 2 * T, (duo + 1) * 2 * T)
            upper, lower = by_rows[row : row + T, lanes], by_rows[row + T : row + 2 * T, lanes]
            first = jnp.where(low, upper, swap_halves(lower))
            other = jnp.where(low, swap_halves(upper), lower)
            at = 2 * duo * T
            return (
                first + by_cols[at : at + T, row : row + 2 * T],
                other + by_cols[at + T : at + 2 * T, row : row + 2 * T],
            )

        for two in range(2):
            evens = tiles_of(2 * two, 0) + tiles_of(2 * two, 1)
            odds = tiles_of(2 * two + 1, 0) + tiles_of(2 * two + 1, 1)
            at = pl.ds(pl.multiple_of((step * 4 + 2 * two) * 8, 16), 16)
            for d, (even, odd) in enumerate(zip(evens, odds)):
                if d == 0:
                    tiles = [
                        skewed(jnp.where(low, even, swap_halves(odd))),
                        skewed(jnp.where(low, swap_halves(even), odd)),
                    ]
                else:
                    first, second_tile = skewed(even), skewed(odd)
                    tiles = [(first[half], second_tile[half]) for half in range(2)]
                for half in range(2):
                    for j in range(4):
                        part = lax.rem(step // 2 + j, 4)
                        index = part * 4 + d if half == 0 else d * 4 + part
                        rows16 = jnp.concatenate([tiles[half][0][j], tiles[half][1][j]], axis=0)
                        out[half, index, at, :] = rows16.astype(BF16)
        return 0

    lax.fori_loop(0, 8, group, 0, unroll=8)


def terms(rel, triples, blocks, panels):
    vmem = pl.BlockSpec(memory_space=pltpu.VMEM)
    return pl.pallas_call(
        functools.partial(terms_kernel, rel),
        out_shape=jax.ShapeDtypeStruct((2, 16, 256, 2 * T), BF16),
        in_specs=[pl.BlockSpec(memory_space=pltpu.SMEM)] + [vmem] * 6,
        out_specs=vmem,
        scratch_shapes=[pltpu.VMEM((BLOCK_ROWS, 4 * T), BF16)],
        compiler_params=pltpu.CompilerParams(vmem_limit_bytes=VMEM_LIMIT),
        cost_estimate=pl.CostEstimate(flops=1 << 31, bytes_accessed=5 << 20, transcendentals=0),
        name="terms",
    )(triples, *blocks, panels)


def add_kernel(keep, got, small, first, *second):
    for half, outs in ((0, [first]), (1, second)):
        per_out = 16 // len(outs)
        for at, out in enumerate(outs):

            def one(index, _):
                source = at * per_out + index
                total = keep[half, source].astype(F32) + got[half, source].astype(F32)
                out[pl.ds(pl.multiple_of(index * 256, 256), 256), :] = total.astype(BF16)
                return 0

            lax.fori_loop(0, per_out, one, 0, unroll=4)
    for out in second[1:]:
        out[1024:, :] = small[...]


def add(keep, got, small):
    vmem = pl.BlockSpec(memory_space=pltpu.VMEM)

    def rows(count):
        return jax.ShapeDtypeStruct((count, 2 * T), BF16)

    return pl.pallas_call(
        add_kernel,
        out_shape=(rows(4096), rows(1024)) + (rows(1024 + SMALL_ROWS),) * 3,
        in_specs=[vmem] * 3,
        out_specs=[vmem] * 5,
        compiler_params=pltpu.CompilerParams(vmem_limit_bytes=VMEM_LIMIT),
        name="add",
    )(keep, got, small)


def gather_terms(mid_is_j, one, two, three, by_j, by_i):
    middle = two.astype(F32)
    by_j[...] = one.astype(F32) + jnp.where(mid_is_j, middle, 0.0)
    by_i[...] = three.astype(F32) + jnp.where(mid_is_j, 0.0, middle)


def lane_key(part, rows, lanes):
    quarter = lax.broadcasted_iota(jnp.int32, (rows, lanes), 1) // 8
    return jnp.bitwise_and(part + 4 * 64 - quarter, 3)


def by_key(key, options, shift):
    value = options[(3 - shift) % 4]
    for k in (2, 1, 0):
        value = jnp.where(key == k, options[(k - shift) % 4], value)
    return value


def own_tile(load, key, q):
    groups = []
    pairs = [load((c_quarter * 4 + q) * 16).astype(F32) for c_quarter in range(4)]
    for half in range(2):
        options = [x[half * 8 : half * 8 + 8] for x in pairs]
        groups += [by_key(key, options, b_quarter) for b_quarter in range(4)]
    return jnp.concatenate(groups, axis=0)


def turned_sum(own, by_j, by_i, base, q):
    low = lane_low(H)

    def as_rows(table):
        even = table[pl.ds(base + 2 * q, H, stride=8), :]
        odd = table[pl.ds(base + 2 * q + 1, H, stride=8), :]
        top = jnp.where(low, even, swap_halves(odd))
        bottom = jnp.where(low, swap_halves(even), odd)
        return jnp.concatenate([top, bottom], axis=0)

    flat = as_rows(by_i).T
    return own + as_rows(by_j) + jnp.concatenate([flat[:T], flat[T:]], axis=1)


def middle_is_j(triples):
    core = lax.rem(lax.axis_index("virt"), 2)
    _, off_j, _ = row_of(triples, lax.axis_index("trip"), core, 0)
    return off_j == 2


def combine_kernel(triples, own, one, two, three, out, by_j, by_i):
    rows = pl.ds(0, 1024)
    gather_terms(middle_is_j(triples), one[rows, :], two[rows, :], three[rows, :], by_j, by_i)
    for part in range(4):
        key = lane_key(part, 8, 2 * T)
        for q in range(4):
            tile = own_tile(lambda at: own[part * 256 + at : part * 256 + at + 16, :], key, q)
            total = turned_sum(tile, by_j, by_i, part * 256, q)
            out[part, q * T : (q + 1) * T, :] = total.astype(BF16)


def combine(triples, own, one, two, three):
    vmem = pl.BlockSpec(memory_space=pltpu.VMEM)
    return pl.pallas_call(
        combine_kernel,
        out_shape=jax.ShapeDtypeStruct((4, 256, 2 * T), BF16),
        in_specs=[pl.BlockSpec(memory_space=pltpu.SMEM)] + [vmem] * 4,
        out_specs=vmem,
        scratch_shapes=[pltpu.VMEM((1024, 2 * T), F32)] * 2,
        compiler_params=pltpu.CompilerParams(vmem_limit_bytes=VMEM_LIMIT),
        name="combine",
    )(triples, own, one, two, three)


PART_PITCH = T + 8
PART_ROWS = 16 * PART_PITCH


def energy_kernel(
    triples, own, one, two, three, others, extra_b, extra_a, inverse, out, by_j, by_i, plain, turned
):
    virt = lax.axis_index("virt")
    _, _, live = row_of(triples, lax.axis_index("trip"), lax.rem(virt, 2), 0)
    gather_terms(middle_is_j(triples), one[...], two[...], three[...], by_j, by_i)
    wide_key = lane_key(virt // 2, 8, 2 * T)
    key = lane_key(virt // 2, 8, T)
    for q in range(4):
        at = slice(q * T, (q + 1) * T)
        tile = own_tile(lambda at: own[at : at + 16, :], wide_key, q)
        first = turned_sum(tile, by_j, by_i, 0, q)
        second = sum(others[source, at, :].astype(F32) for source in range(4))
        for half, tile in ((0, first), (1, second)):
            base = (half * 8 + 2 * q) * PART_PITCH
            flat = tile.T
            plain[base : base + T, :] = tile[:, :T]
            turned[base : base + T, :] = flat[:T]
            base += PART_PITCH
            plain[base : base + T, :] = swap_halves(tile)[:, :T]
            turned[base : base + T, :] = flat[T:]

    def exchanged(table, half, c_low):
        groups = []
        for b_half in range(2):
            options = [
                table[
                    pl.ds(b_half * 8 * PART_PITCH + half * H + 8 * at + c_low, 8, stride=PART_PITCH), :
                ]
                for at in range(4)
            ]
            groups += [by_key(key, options, b_quarter) for b_quarter in range(4)]
        return jnp.concatenate(groups, axis=0)

    sum_b = jnp.zeros((T, T), F32)
    sum_a = jnp.zeros((T, T), F32)
    for half in range(2):
        for c_low in range(8):
            index = half * 8 + c_low
            at = slice(index * T, (index + 1) * T)
            acb = exchanged(plain, half, c_low)
            cab = exchanged(turned, half, c_low)
            bac = turned[index * PART_PITCH : index * PART_PITCH + T, :]
            inv = inverse[at, :]
            sum_b += (4.0 * bac + acb) * (bac - cab + extra_b[at, :]) * inv
            sum_a += bac * (acb - acb.T + extra_a[at, :]) * inv
    total = jnp.sum(sum_a + sum_b.T, axis=0, keepdims=True)
    total = jnp.where(live, total, 0.0)
    total = jnp.concatenate([total, jnp.zeros_like(total)], axis=1)
    out[...] = jnp.broadcast_to(total[None], out.shape)


def energy_of(triples, own, shares, others, extra_b, extra_a, inverse):
    vmem = pl.BlockSpec(memory_space=pltpu.VMEM)
    return pl.pallas_call(
        energy_kernel,
        out_shape=jax.ShapeDtypeStruct((8, 8, 2 * T), F32),
        in_specs=[pl.BlockSpec(memory_space=pltpu.SMEM)] + [vmem] * 8,
        out_specs=vmem,
        scratch_shapes=[pltpu.VMEM((256, 2 * T), F32)] * 2 + [pltpu.VMEM((PART_ROWS, T), F32)] * 2,
        compiler_params=pltpu.CompilerParams(vmem_limit_bytes=VMEM_LIMIT),
        name="energy",
    )(triples, own, *shares, others, extra_b, extra_a, inverse)


def tables_kernel(
    triples, own, one, two, three, virt_energy, extra_b, extra_a, inverse, columns, rows, matrices
):
    virt = lax.axis_index("virt")
    off_i, off_j, _ = row_of(triples, lax.axis_index("trip"), lax.rem(virt, 2), 0)
    part = virt // 2

    def small_of(table):
        return table[table.shape[0] - SMALL_ROWS :, :]

    def exch(slot, table, index):
        flat = small_of(table)[index * H : (index + 1) * H, :].astype(F32)
        matrices[pl.ds(slot * T, H, stride=2), :] = flat[:, :T]
        matrices[pl.ds(slot * T + 1, H, stride=2), :] = swap_halves(flat)[:, :T]
        return matrices[slot * T : (slot + 1) * T, :]

    def pick(options, index):
        result = options[-1]
        for at in range(len(options) - 1):
            result = jnp.where(index == at, options[at], result)
        return result

    own_exch = [exch(slot, own, slot) for slot in range(3)]
    kj = pick(own_exch[:2], off_j - 1)
    ki = pick(own_exch[1:], off_i - 2)
    ji = pick([exch(3, one, 0), exch(4, one, 1), exch(5, two, 0)], off_i + off_j - 3)
    kj_t, ki_t, ji_t = kj.T, ki.T, ji.T
    heads = [small_of(x)[3 * H :, :].astype(F32) for x in (own, one, two, three)]
    head_i = pick([heads[2], heads[3]], off_i - 2)
    head_j = pick([heads[1], heads[2]], off_j - 1)
    head_k = heads[0]
    occ = head_i[0:1, T:] + head_j[0:1, T:] + head_k[0:1, T:]
    s_i, s_j, s_k = (x[0:1, :T] for x in (head_i, head_j, head_k))
    e_a = virt_energy[...]
    s_ib, s_jb, s_kb, e_b = (jnp.broadcast_to(v, (T, T)).T for v in (s_i, s_j, s_k, e_a))
    for at, m in enumerate((kj, ji_t, ji, kj_t, s_ib, s_jb, s_kb, e_b)):
        rows[at * T : (at + 1) * T, :] = m
    for at, m in enumerate((kj, ji_t, ki_t, ki)):
        for half in range(2):
            for quarter in range(4):
                base = quarter * T + at * 16 + half * 8
                source = half * H + quarter * 8
                columns[base : base + 8, :] = m[source : source + 8]
    key = lane_key(part, 1, T)
    key_rows = lane_key(part, T, T)
    c_of_row = lax.broadcasted_iota(jnp.int32, (T, T), 0)
    ki_diff = ki - ki_t

    def one(index, _):
        half, c_low = index // 8, lax.rem(index, 8)
        first_c = half * H + c_low
        looked_up = [
            [rows[pl.ds(at * T + first_c + 8 * quarter, 1), :] for quarter in range(4)]
            for at in range(8)
        ]
        for quarter in range(4):
            wanted = first_c + 8 * jnp.bitwise_and(key_rows - quarter, 3)
            choice = jnp.where(c_of_row == wanted, 1.0, 0.0).astype(BF16)
            source = columns[quarter * T : (quarter + 1) * T, :].astype(BF16)
            over_bc = jnp.dot(source, choice, preferred_element_type=F32)
            kj_ca, ji_ac, ji_ca, kj_ac, si_c, sj_c, sk_c, e_c = (
                by_key(key, options, quarter) for options in looked_up
            )
            for b_half in range(2):
                at = b_half * H + quarter * 8
                b = slice(at, at + 8)
                kj_bc, ji_cb, ki_cb, ki_bc = (
                    over_bc[g * 16 + b_half * 8 : g * 16 + b_half * 8 + 8] for g in range(4)
                )
                target = pl.ds(pl.multiple_of(index * T + at, 8), 8)
                extra_b[target, :] = (
                    s_ib[b] * kj_ca
                    - s_kb[b] * ji_ac
                    + s_j * (ki_cb - ki_bc)
                    + sk_c * ji_t[b]
                    - si_c * kj[b]
                )
                extra_a[target, :] = (
                    s_kb[b] * ji_ca
                    - s_ib[b] * kj_ac
                    + s_i * kj_bc
                    - s_k * ji_cb
                    + sj_c * ki_diff[b]
                )
                inverse[target, :] = 1.0 / (occ - e_a - e_b[b] - e_c)
        return 0

    lax.fori_loop(0, 16, one, 0, unroll=2)


def tables(triples, small, virt_energy):
    vmem = pl.BlockSpec(memory_space=pltpu.VMEM)
    table = jax.ShapeDtypeStruct((16 * T, T), F32)
    return pl.pallas_call(
        tables_kernel,
        out_shape=(table, table, table),
        in_specs=[pl.BlockSpec(memory_space=pltpu.SMEM)] + [vmem] * 5,
        out_specs=[vmem] * 3,
        scratch_shapes=[pltpu.VMEM((rows * T, T), F32) for rows in (4, 8, 6)],
        compiler_params=pltpu.CompilerParams(vmem_limit_bytes=VMEM_LIMIT),
        cost_estimate=pl.CostEstimate(flops=1 << 28, bytes_accessed=3 << 20, transcendentals=0),
        name="tables",
    )(triples, *small, virt_energy)


def local(
    virt_integrals,
    pair_amps,
    hole_amps,
    coulomb_ints,
    exchange_ints,
    singles,
    occ_energy,
    virt_energy,
    triples,
):
    n_trip = lax.axis_size("trip")

    out1, out2, out3, up1, up2 = prep(
        triples, pair_amps.reshape(3, 2 * T, 4 * T), coulomb_ints.reshape(coulomb_ints.shape[1:])
    )
    got_two = lax.ppermute(up2, "trip", shift_route(n_trip, -2))
    in2 = lax.ppermute(out2, "trip", shift_route(n_trip, 2))
    got_one = lax.ppermute(up1, "trip", shift_route(n_trip, -1))
    in1 = lax.ppermute(out1, "trip", shift_route(n_trip, 1))
    in3 = lax.ppermute(out3, "trip", shift_route(n_trip, 3))
    blocks = (got_one, got_two, in1, in2, in3)

    panels = panels_of(
        virt_integrals.reshape(4 * T, T * T), hole_amps.reshape(hole_amps.shape[1:])
    )

    heads = jnp.concatenate([singles, jnp.broadcast_to(occ_energy[:, None], (1, T))], axis=1)
    small = jnp.concatenate(
        [exchange_ints.reshape(3 * H, 2 * T), heads, jnp.zeros((15, 2 * T), BF16)], axis=0
    )
    panels, small = lax.optimization_barrier((panels, small))

    send = terms(1, triples, blocks, panels)
    got = lax.ppermute(send, "virt", CORE_ROUTE)
    keep = terms(0, triples, blocks, panels)
    first_half, *second_half = add(keep, got, small)
    over_y = functools.partial(
        lax.all_to_all,
        axis_name="virt",
        split_axis=0,
        concat_axis=0,
        axis_index_groups=[[0, 2, 4, 6], [1, 3, 5, 7]],
        tiled=True,
    )
    by_y = over_y(first_half.reshape(16, 256, 2 * T))
    by_owner = [
        lax.ppermute(second_half[d], "trip", shift_route(n_trip, -d)) for d in (1, 2, 3)
    ]

    total = by_y.reshape(4, 4, 256, 2 * T).astype(F32)
    total = total[0] + total[1] + total[2] + total[3]
    to_share = [total[d].astype(BF16) for d in (1, 2, 3)]
    shares = [
        lax.ppermute(to_share[d - 1], "trip", shift_route(n_trip, -d)) for d in (1, 2, 3)
    ]
    by_owner, _ = lax.optimization_barrier((by_owner, to_share))
    others = over_y(combine(triples, second_half[0], *by_owner))
    extras = tables(triples, [small, *by_owner], virt_energy.reshape(1, T))

    mine = energy_of(triples, total[0], shares, others, *extras)
    everyone = lax.all_to_all(mine, "virt", 0, 0, tiled=True)
    return jnp.sum(everyone[:, 0, :T].reshape(4, 2, T), axis=0)


def solution(mesh):
    placed = (
        P("trip", "virt", None),
        P("trip", None, None, None, "virt"),
        P("trip", "virt", None),
        P("trip", None, "virt", None),
        P("trip", None, None),
        P("trip", None),
        P("trip"),
        P(),
        P("trip", None),
    )
    return jax.shard_map(
        local, mesh=mesh, in_specs=placed, out_specs=P("trip", None), check_vma=False
    )
```

```python
import functools

import jax
import jax.numpy as jnp
from jax import lax
from jax.experimental import pallas as pl
from jax.experimental.pallas import tpu as pltpu
from jax.sharding import PartitionSpec as P

T = 64
H = 32
F32 = jnp.float32
BF16 = jnp.bfloat16
CROWS = 16
BLOCK_ROWS = 2 * T + CROWS
SMALL_ROWS = 3 * H + 16
VMEM_LIMIT = 12 * 1024 * 1024


def shift_route(size, distance):
    return [(i, i + distance) for i in range(size) if 0 <= i + distance < size]


CORE_ROUTE = [(i, i ^ 1) for i in range(8)]


def in_hbm(array):
    return pltpu.with_memory_space_constraint(array, pltpu.HBM)


def lane_low(rows):
    return lax.broadcasted_iota(jnp.int32, (rows, 2 * T), 1) < T


def swap_halves(x):
    return pltpu.roll(x, T, 1)


def row_of(triples, owner, core, rel):
    s = jnp.where(core == 0, rel, 1 - rel)
    live = triples[s, 0] >= 0
    off_i = jnp.where(live, triples[s, 0] - owner, 2)
    off_j = jnp.where(live, triples[s, 1] - owner, 1)
    return off_i, off_j, live


def prep_kernel(triples, amps, coulomb, out1, out2, out3, up1, up2, blocks):
    owner, core = lax.axis_index("trip"), lax.rem(lax.axis_index("virt"), 2)
    occ_rows = coulomb.shape[1]
    for s in range(3):
        blocks[s, : 2 * T, :] = amps[s]
        turned = jnp.concatenate(
            [coulomb[s].astype(F32), jnp.zeros((T - occ_rows, T), F32)], axis=0
        ).T
        packed = jnp.concatenate([-turned[g * CROWS : (g + 1) * CROWS] for g in range(4)], axis=1)
        blocks[s, 2 * T :, :] = packed.astype(BF16)
    up1[...] = blocks[0:2]
    up2[...] = blocks[0]
    for rel in range(2):
        off_i, off_j, live = row_of(triples, owner, core, rel)
        for d, out in ((1, out1), (2, out2), (3, out3)):
            takes_part = live & ((off_i == d) | (off_j == d))
            other = jnp.clip(off_i + off_j - d - 1, 0, 2)

            @pl.when(takes_part)
            def _():
                out[rel] = blocks[other]

            @pl.when(jnp.logical_not(takes_part))
            def _():
                out[rel] = jnp.zeros((BLOCK_ROWS, 4 * T), BF16)


def prep(triples, amps, coulomb):
    vmem = pl.BlockSpec(memory_space=pltpu.VMEM)
    two = jax.ShapeDtypeStruct((2, BLOCK_ROWS, 4 * T), BF16)
    one = jax.ShapeDtypeStruct((BLOCK_ROWS, 4 * T), BF16)
    return pl.pallas_call(
        prep_kernel,
        out_shape=(two, two, two, two, one),
        in_specs=[pl.BlockSpec(memory_space=pltpu.SMEM), pl.BlockSpec(), pl.BlockSpec()],
        out_specs=[vmem] * 5,
        scratch_shapes=[
            pltpu.VMEM((3, BLOCK_ROWS, 4 * T), BF16),
        ],
        compiler_params=pltpu.CompilerParams(vmem_limit_bytes=VMEM_LIMIT),
        name="prep",
    )(triples, in_hbm(amps), in_hbm(coulomb))


STEPS = 8
DEPTH = 6 * T
PITCH = 2 * T + 8


def panels_kernel(integrals_in, holes, out, spread_a, spread_b, integrals, sems):
    occ_rows = holes.shape[0]
    per_step = H // STEPS
    width = per_step * 2 * T
    copies = []
    for step in range(STEPS):
        span = pl.ds(step * width, width)
        copies.append(
            pltpu.make_async_copy(integrals_in.at[:, span], integrals.at[:, span], sems.at[step])
        )
    for copy in copies:
        copy.start()
    for step in range(STEPS):
        copies[step].wait()
        for chunk in range(step * per_step, (step + 1) * per_step):
            columns = slice(chunk * 2 * T, (chunk + 1) * 2 * T)
            turned = integrals[:, columns].astype(F32).T
            for part in range(4):
                at = pl.ds((part % 2) * T + chunk * 2 + part // 2, H, stride=PITCH)
                spread_a[at, :] = turned[part * H : (part + 1) * H, : 2 * T]
                spread_b[at, :] = turned[part * H : (part + 1) * H, 2 * T :]
    for chunk in range(H):
        hole = holes[:, chunk * 2 * T : (chunk + 1) * 2 * T].astype(F32)
        hole = jnp.concatenate([hole, jnp.zeros((2 * T - occ_rows, 2 * T), F32)], axis=0).T
        for w in range(2):
            third = chunk * 2 + w
            at = third % H * 2 * T + third // H * T
            out[at : at + T, 4 * T :] = hole[w * T : (w + 1) * T].astype(BF16)

    def settle(step, _):
        rows = pl.ds(pl.multiple_of(step * 2 * T, 2 * T), 2 * T)
        source = pl.ds(pl.multiple_of(step * PITCH, 8), 2 * T)
        out[rows, : 2 * T] = spread_a[source, :].astype(BF16)
        out[rows, 2 * T : 4 * T] = spread_b[source, :].astype(BF16)
        return 0

    lax.fori_loop(0, H, settle, 0, unroll=32)


def panels_of(integrals, holes):
    return pl.pallas_call(
        panels_kernel,
        out_shape=jax.ShapeDtypeStruct((T * T, DEPTH), BF16),
        in_specs=[pl.BlockSpec(memory_space=pltpu.HBM), pl.BlockSpec()],
        out_specs=pl.BlockSpec(memory_space=pltpu.VMEM),
        scratch_shapes=[pltpu.VMEM((H * PITCH, 2 * T), F32)] * 2
        + [
            pltpu.VMEM(integrals.shape, BF16),
            pltpu.SemaphoreType.DMA((STEPS,)),
        ],
        compiler_params=pltpu.CompilerParams(vmem_limit_bytes=VMEM_LIMIT),
        cost_estimate=pl.CostEstimate(flops=1 << 28, bytes_accessed=5 << 20, transcendentals=0),
        name="panels",
    )(in_hbm(integrals), in_hbm(holes))


def terms_kernel(rel, triples, got_one, got_two, in1, in2, in3, panels, out, chosen):
    core = lax.rem(lax.axis_index("virt"), 2)
    off_i, off_j, live = row_of(triples, lax.axis_index("trip"), core, rel)
    which = jnp.where(live, off_i + off_j - 3, 3)
    for at, option in enumerate((got_one.at[0], got_one.at[1], got_two)):

        @pl.when(which == at)
        def _():
            chosen[...] = option[...]

    @pl.when(which == 3)
    def _():
        chosen[...] = jnp.zeros_like(chosen)

    blocks = (chosen, in1.at[rel], in2.at[rel], in3.at[rel])
    lead, second = [], []
    for d in range(4):
        block = blocks[d][...]
        packed = block[2 * T :]
        coulomb = jnp.concatenate(
            [packed[:, g * T : (g + 1) * T] for g in range(4)], axis=0
        )
        coulomb = jnp.concatenate([coulomb, jnp.zeros_like(coulomb)], axis=1)
        lead.append(jnp.concatenate([block[:T], coulomb], axis=1))
        second.append(jnp.concatenate([block[T : 2 * T], coulomb], axis=1))
    lead = jnp.concatenate(lead, axis=0)
    second = jnp.concatenate(second, axis=0).astype(F32).T.astype(BF16)
    low = lane_low(T)
    contract = (((1,), (1,)), ((), ()))

    eighth = lax.broadcasted_iota(jnp.int32, (8, 2 * T), 1) // 8
    odd_eighth = jnp.bitwise_and(eighth, 1) == 1
    high_eighth = jnp.bitwise_and(eighth, 2) == 2

    def skewed(tile):
        result = []
        for half in range(2):
            rows = [tile[half * H + 8 * at : half * H + 8 * at + 8] for at in range(4)]
            rows = [jnp.where(odd_eighth, rows[(j - 1) % 4], rows[j]) for j in range(4)]
            result.append([jnp.where(high_eighth, rows[(j - 2) % 4], rows[j]) for j in range(4)])
        return result

    def group(step, _):
        panel = panels[pl.ds(pl.multiple_of(step * 8 * T, 8 * T), 8 * T), :]
        by_rows = jnp.dot(panel, second, preferred_element_type=F32)
        by_cols = lax.dot_general(lead, panel, contract, preferred_element_type=F32)

        def tiles_of(pair, duo):
            row = pair * 2 * T
            lanes = slice(duo * 2 * T, (duo + 1) * 2 * T)
            upper, lower = by_rows[row : row + T, lanes], by_rows[row + T : row + 2 * T, lanes]
            first = jnp.where(low, upper, swap_halves(lower))
            other = jnp.where(low, swap_halves(upper), lower)
            at = 2 * duo * T
            return (
                first + by_cols[at : at + T, row : row + 2 * T],
                other + by_cols[at + T : at + 2 * T, row : row + 2 * T],
            )

        for two in range(2):
            evens = tiles_of(2 * two, 0) + tiles_of(2 * two, 1)
            odds = tiles_of(2 * two + 1, 0) + tiles_of(2 * two + 1, 1)
            at = pl.ds(pl.multiple_of((step * 4 + 2 * two) * 8, 16), 16)
            for d, (even, odd) in enumerate(zip(evens, odds)):
                if d == 0:
                    tiles = [
                        skewed(jnp.where(low, even, swap_halves(odd))),
                        skewed(jnp.where(low, swap_halves(even), odd)),
                    ]
                else:
                    first, second_tile = skewed(even), skewed(odd)
                    tiles = [(first[half], second_tile[half]) for half in range(2)]
                for half in range(2):
                    for j in range(4):
                        part = lax.rem(step // 2 + j, 4)
                        index = part * 4 + d if half == 0 else d * 4 + part
                        rows16 = jnp.concatenate([tiles[half][0][j], tiles[half][1][j]], axis=0)
                        out[half, index, at, :] = rows16.astype(BF16)
        return 0

    lax.fori_loop(0, 8, group, 0, unroll=8)


def terms(rel, triples, blocks, panels):
    vmem = pl.BlockSpec(memory_space=pltpu.VMEM)
    return pl.pallas_call(
        functools.partial(terms_kernel, rel),
        out_shape=jax.ShapeDtypeStruct((2, 16, 256, 2 * T), BF16),
        in_specs=[pl.BlockSpec(memory_space=pltpu.SMEM)] + [vmem] * 6,
        out_specs=vmem,
        scratch_shapes=[pltpu.VMEM((BLOCK_ROWS, 4 * T), BF16)],
        compiler_params=pltpu.CompilerParams(vmem_limit_bytes=VMEM_LIMIT),
        cost_estimate=pl.CostEstimate(flops=1 << 31, bytes_accessed=5 << 20, transcendentals=0),
        name="terms",
    )(triples, *blocks, panels)


def add_kernel(keep, got, exchange, singles, occ, first, own, one, two, three, small, table):
    for s in range(3):
        for row in range(H):
            lanes = slice(row * 2 * T, (row + 1) * 2 * T)
            table[s * H + row : s * H + row + 1, :] = exchange[s : s + 1, lanes].astype(F32)
    heads = [singles[...].astype(F32), jnp.broadcast_to(occ[...].astype(F32), (1, T))]
    table[3 * H :, :] = jnp.broadcast_to(jnp.concatenate(heads, axis=1), (16, 2 * T))
    small[...] = table[...].astype(BF16)
    second = (own, one, two, three)
    for half, outs in ((0, [first]), (1, second)):
        per_out = 16 // len(outs)
        for at, out in enumerate(outs):

            def one(index, _):
                source = at * per_out + index
                total = keep[half, source].astype(F32) + got[half, source].astype(F32)
                out[pl.ds(pl.multiple_of(index * 256, 256), 256), :] = total.astype(BF16)
                return 0

            lax.fori_loop(0, per_out, one, 0, unroll=4)
    for out in second[1:]:
        out[1024:, :] = small[...]


def add(keep, got, exchange, singles, occ):
    vmem = pl.BlockSpec(memory_space=pltpu.VMEM)

    def rows(count):
        return jax.ShapeDtypeStruct((count, 2 * T), BF16)

    return pl.pallas_call(
        add_kernel,
        out_shape=(rows(4096), rows(1024))
        + (rows(1024 + SMALL_ROWS),) * 3
        + (rows(SMALL_ROWS),),
        in_specs=[vmem] * 5,
        out_specs=[vmem] * 6,
        scratch_shapes=[pltpu.VMEM((SMALL_ROWS, 2 * T), F32)],
        compiler_params=pltpu.CompilerParams(vmem_limit_bytes=VMEM_LIMIT),
        name="add",
    )(keep, got, exchange, singles, occ)


def collect_kernel(by_y, out):
    for d in range(4):
        out[d] = sum(by_y[source * 4 + d].astype(F32) for source in range(4))


def collect(by_y):
    vmem = pl.BlockSpec(memory_space=pltpu.VMEM)
    return pl.pallas_call(
        collect_kernel,
        out_shape=jax.ShapeDtypeStruct((4, 256, 2 * T), F32),
        in_specs=[vmem],
        out_specs=vmem,
        compiler_params=pltpu.CompilerParams(vmem_limit_bytes=VMEM_LIMIT),
        name="collect",
    )(by_y)


def gather_terms(mid_is_j, one, two, three, by_j, by_i):
    middle = two.astype(F32)
    by_j[...] = one.astype(F32) + jnp.where(mid_is_j, middle, 0.0)
    by_i[...] = three.astype(F32) + jnp.where(mid_is_j, 0.0, middle)


def lane_key(part, rows, lanes):
    quarter = lax.broadcasted_iota(jnp.int32, (rows, lanes), 1) // 8
    return jnp.bitwise_and(part + 4 * 64 - quarter, 3)


def by_key(key, options, shift):
    value = options[(3 - shift) % 4]
    for k in (2, 1, 0):
        value = jnp.where(key == k, options[(k - shift) % 4], value)
    return value


def own_tile(load, key, q):
    groups = []
    pairs = [load((c_quarter * 4 + q) * 16).astype(F32) for c_quarter in range(4)]
    for half in range(2):
        options = [x[half * 8 : half * 8 + 8] for x in pairs]
        groups += [by_key(key, options, b_quarter) for b_quarter in range(4)]
    return jnp.concatenate(groups, axis=0)


def turned_sums(owns, by_j, by_i, base, q):
    low, low_rows = lane_low(H), lane_low(T)

    def as_rows(table, q):
        even = table[pl.ds(base + 2 * q, H, stride=8), :]
        odd = table[pl.ds(base + 2 * q + 1, H, stride=8), :]
        top = jnp.where(low, even, swap_halves(odd))
        bottom = jnp.where(low, swap_halves(even), odd)
        return jnp.concatenate([top, bottom], axis=0)

    flat = jnp.concatenate([as_rows(by_i, q), as_rows(by_i, q + 1)], axis=0).T
    first, second = flat[:T], flat[T:]
    return (
        owns[0] + as_rows(by_j, q) + jnp.where(low_rows, first, swap_halves(second)),
        owns[1] + as_rows(by_j, q + 1) + jnp.where(low_rows, swap_halves(first), second),
    )


def middle_is_j(triples):
    core = lax.rem(lax.axis_index("virt"), 2)
    _, off_j, _ = row_of(triples, lax.axis_index("trip"), core, 0)
    return off_j == 2


def combine_kernel(triples, own, one, two, three, out, by_j, by_i):
    rows = pl.ds(0, 1024)
    gather_terms(middle_is_j(triples), one[rows, :], two[rows, :], three[rows, :], by_j, by_i)
    for part in range(4):
        key = lane_key(part, 8, 2 * T)

        def load(at):
            return own[part * 256 + at : part * 256 + at + 16, :]

        for q in (0, 2):
            owns = [own_tile(load, key, q), own_tile(load, key, q + 1)]
            for at, total in enumerate(turned_sums(owns, by_j, by_i, part * 256, q)):
                out[part, (q + at) * T : (q + at + 1) * T, :] = total.astype(BF16)


def combine(triples, own, one, two, three):
    vmem = pl.BlockSpec(memory_space=pltpu.VMEM)
    return pl.pallas_call(
        combine_kernel,
        out_shape=jax.ShapeDtypeStruct((4, 256, 2 * T), BF16),
        in_specs=[pl.BlockSpec(memory_space=pltpu.SMEM)] + [vmem] * 4,
        out_specs=vmem,
        scratch_shapes=[pltpu.VMEM((1024, 2 * T), F32)] * 2,
        compiler_params=pltpu.CompilerParams(vmem_limit_bytes=VMEM_LIMIT),
        name="combine",
    )(triples, own, one, two, three)


PART_PITCH = T + 8
PART_ROWS = 16 * PART_PITCH


def energy_kernel(
    triples, own, one, two, three, others, extra_b, extra_a, inverse, out, by_j, by_i, plain, turned
):
    virt = lax.axis_index("virt")
    _, _, live = row_of(triples, lax.axis_index("trip"), lax.rem(virt, 2), 0)
    gather_terms(middle_is_j(triples), one[...], two[...], three[...], by_j, by_i)
    wide_key = lane_key(virt // 2, 8, 2 * T)
    key = lane_key(virt // 2, 8, T)
    for q in range(4):
        if q % 2 == 0:
            owns = [own_tile(lambda at: own[at : at + 16, :], wide_key, q + at) for at in range(2)]
            firsts = turned_sums(owns, by_j, by_i, 0, q)
        first = firsts[q % 2]
        at = slice(q * T, (q + 1) * T)
        second = sum(others[source, at, :].astype(F32) for source in range(4))
        flat = jnp.concatenate([first, second], axis=0).T
        flat_swapped = swap_halves(flat)
        for half, tile, across in ((0, first, flat), (1, second, flat_swapped)):
            base = (half * 8 + 2 * q) * PART_PITCH
            plain[base : base + T, :] = tile[:, :T]
            turned[base : base + T, :] = across[:T, :T]
            base += PART_PITCH
            plain[base : base + T, :] = swap_halves(tile)[:, :T]
            turned[base : base + T, :] = across[T:, :T]

    def exchanged(table, half, c_low):
        groups = []
        for b_half in range(2):
            options = [
                table[
                    pl.ds(b_half * 8 * PART_PITCH + half * H + 8 * at + c_low, 8, stride=PART_PITCH), :
                ]
                for at in range(4)
            ]
            groups += [by_key(key, options, b_quarter) for b_quarter in range(4)]
        return jnp.concatenate(groups, axis=0)

    sum_b = jnp.zeros((T, T), F32)
    sum_a = jnp.zeros((T, T), F32)
    for c_low in range(8):
        acbs = [exchanged(plain, half, c_low) for half in range(2)]
        flat = jnp.concatenate(acbs, axis=1).T
        for half, acb in enumerate(acbs):
            index = half * 8 + c_low
            at = slice(index * T, (index + 1) * T)
            cab = exchanged(turned, half, c_low)
            bca = flat[half * T : (half + 1) * T]
            bac = turned[index * PART_PITCH : index * PART_PITCH + T, :]
            inv = inverse[at, :]
            sum_b += (4.0 * bac + acb) * (bac - cab + extra_b[at, :]) * inv
            sum_a += bac * (acb - bca + extra_a[at, :]) * inv
    total = jnp.sum(sum_a + sum_b.T, axis=0, keepdims=True)
    total = jnp.where(live, total, 0.0)
    total = jnp.concatenate([total, jnp.zeros_like(total)], axis=1)
    out[...] = jnp.broadcast_to(total[None], out.shape)


def energy_of(triples, own, shares, others, extra_b, extra_a, inverse):
    vmem = pl.BlockSpec(memory_space=pltpu.VMEM)
    return pl.pallas_call(
        energy_kernel,
        out_shape=jax.ShapeDtypeStruct((8, 8, 2 * T), F32),
        in_specs=[pl.BlockSpec(memory_space=pltpu.SMEM)] + [vmem] * 8,
        out_specs=vmem,
        scratch_shapes=[pltpu.VMEM((256, 2 * T), F32)] * 2 + [pltpu.VMEM((PART_ROWS, T), F32)] * 2,
        compiler_params=pltpu.CompilerParams(vmem_limit_bytes=VMEM_LIMIT),
        name="energy",
    )(triples, own, *shares, others, extra_b, extra_a, inverse)


def tables_kernel(
    triples, own, one, two, three, virt_energy, extra_b, extra_a, inverse, columns, rows, matrices
):
    virt = lax.axis_index("virt")
    off_i, off_j, _ = row_of(triples, lax.axis_index("trip"), lax.rem(virt, 2), 0)
    part = virt // 2

    def small_of(table):
        return table[table.shape[0] - SMALL_ROWS :, :]

    def exch(slot, table, index):
        flat = small_of(table)[index * H : (index + 1) * H, :].astype(F32)
        matrices[pl.ds(slot * T, H, stride=2), :] = flat[:, :T]
        matrices[pl.ds(slot * T + 1, H, stride=2), :] = swap_halves(flat)[:, :T]
        return matrices[slot * T : (slot + 1) * T, :]

    def pick(options, index):
        result = options[-1]
        for at in range(len(options) - 1):
            result = jnp.where(index == at, options[at], result)
        return result

    own_exch = [exch(slot, own, slot) for slot in range(3)]
    kj = pick(own_exch[:2], off_j - 1)
    ki = pick(own_exch[1:], off_i - 2)
    ji = pick([exch(3, one, 0), exch(4, one, 1), exch(5, two, 0)], off_i + off_j - 3)
    kj_t, ki_t, ji_t = kj.T, ki.T, ji.T
    heads = [small_of(x)[3 * H :, :].astype(F32) for x in (own, one, two, three)]
    head_i = pick([heads[2], heads[3]], off_i - 2)
    head_j = pick([heads[1], heads[2]], off_j - 1)
    head_k = heads[0]
    occ = head_i[0:1, T:] + head_j[0:1, T:] + head_k[0:1, T:]
    s_i, s_j, s_k = (x[0:1, :T] for x in (head_i, head_j, head_k))
    e_a = virt_energy[...]
    s_ib, s_jb, s_kb, e_b = (jnp.broadcast_to(v, (T, T)).T for v in (s_i, s_j, s_k, e_a))
    for at, m in enumerate((kj, ji_t, ji, kj_t, s_ib, s_jb, s_kb, e_b)):
        rows[at * T : (at + 1) * T, :] = m
    for at, m in enumerate((kj, ji_t, ki_t, ki)):
        for half in range(2):
            for quarter in range(4):
                base = quarter * T + at * 16 + half * 8
                source = half * H + quarter * 8
                columns[base : base + 8, :] = m[source : source + 8]
    key = lane_key(part, 1, T)
    key_rows = lane_key(part, T, T)
    c_of_row = lax.broadcasted_iota(jnp.int32, (T, T), 0)
    ki_diff = ki - ki_t

    def one(index, _):
        half, c_low = index // 8, lax.rem(index, 8)
        first_c = half * H + c_low
        looked_up = [
            [rows[pl.ds(at * T + first_c + 8 * quarter, 1), :] for quarter in range(4)]
            for at in range(8)
        ]
        for quarter in range(4):
            wanted = first_c + 8 * jnp.bitwise_and(key_rows - quarter, 3)
            choice = jnp.where(c_of_row == wanted, 1.0, 0.0).astype(BF16)
            source = columns[quarter * T : (quarter + 1) * T, :].astype(BF16)
            over_bc = jnp.dot(source, choice, preferred_element_type=F32)
            kj_ca, ji_ac, ji_ca, kj_ac, si_c, sj_c, sk_c, e_c = (
                by_key(key, options, quarter) for options in looked_up
            )
            for b_half in range(2):
                at = b_half * H + quarter * 8
                b = slice(at, at + 8)
                kj_bc, ji_cb, ki_cb, ki_bc = (
                    over_bc[g * 16 + b_half * 8 : g * 16 + b_half * 8 + 8] for g in range(4)
                )
                target = pl.ds(pl.multiple_of(index * T + at, 8), 8)
                extra_b[target, :] = (
                    s_ib[b] * kj_ca
                    - s_kb[b] * ji_ac
                    + s_j * (ki_cb - ki_bc)
                    + sk_c * ji_t[b]
                    - si_c * kj[b]
                )
                extra_a[target, :] = (
                    s_kb[b] * ji_ca
                    - s_ib[b] * kj_ac
                    + s_i * kj_bc
                    - s_k * ji_cb
                    + sj_c * ki_diff[b]
                )
                inverse[target, :] = 1.0 / (occ - e_a - e_b[b] - e_c)
        return 0

    lax.fori_loop(0, 16, one, 0, unroll=2)


def tables(triples, small, virt_energy):
    vmem = pl.BlockSpec(memory_space=pltpu.VMEM)
    table = jax.ShapeDtypeStruct((16 * T, T), F32)
    return pl.pallas_call(
        tables_kernel,
        out_shape=(table, table, table),
        in_specs=[pl.BlockSpec(memory_space=pltpu.SMEM)] + [vmem] * 5,
        out_specs=[vmem] * 3,
        scratch_shapes=[pltpu.VMEM((rows * T, T), F32) for rows in (4, 8, 6)],
        compiler_params=pltpu.CompilerParams(vmem_limit_bytes=VMEM_LIMIT),
        cost_estimate=pl.CostEstimate(flops=1 << 28, bytes_accessed=3 << 20, transcendentals=0),
        name="tables",
    )(triples, *small, virt_energy)


def local(
    virt_integrals,
    pair_amps,
    hole_amps,
    coulomb_ints,
    exchange_ints,
    singles,
    occ_energy,
    virt_energy,
    triples,
):
    n_trip = lax.axis_size("trip")

    out1, out2, out3, up1, up2 = prep(
        triples, pair_amps.reshape(3, 2 * T, 4 * T), coulomb_ints.reshape(coulomb_ints.shape[1:])
    )
    got_two = lax.ppermute(up2, "trip", shift_route(n_trip, -2))
    in2 = lax.ppermute(out2, "trip", shift_route(n_trip, 2))
    got_one = lax.ppermute(up1, "trip", shift_route(n_trip, -1))
    in1 = lax.ppermute(out1, "trip", shift_route(n_trip, 1))
    in3 = lax.ppermute(out3, "trip", shift_route(n_trip, 3))
    blocks = (got_one, got_two, in1, in2, in3)

    panels = panels_of(
        virt_integrals.reshape(4 * T, T * T), hole_amps.reshape(hole_amps.shape[1:])
    )

    send = terms(1, triples, blocks, panels)
    got = lax.ppermute(send, "virt", CORE_ROUTE)
    keep = terms(0, triples, blocks, panels)
    first_half, *second_half, small = add(
        keep, got, exchange_ints.reshape(3, T * T), singles, occ_energy.reshape(1, 1)
    )
    over_y = functools.partial(
        lax.all_to_all,
        axis_name="virt",
        split_axis=0,
        concat_axis=0,
        axis_index_groups=[[0, 2, 4, 6], [1, 3, 5, 7]],
        tiled=True,
    )
    by_y = over_y(first_half.reshape(16, 256, 2 * T))
    by_owner = [
        lax.ppermute(second_half[d], "trip", shift_route(n_trip, -d)) for d in (1, 2, 3)
    ]

    total = collect(by_y)
    to_share = [total[d].astype(BF16) for d in (1, 2, 3)]
    shares = [
        lax.ppermute(to_share[d - 1], "trip", shift_route(n_trip, -d)) for d in (1, 2, 3)
    ]
    by_owner, _ = lax.optimization_barrier((by_owner, to_share))
    others = over_y(combine(triples, second_half[0], *by_owner))
    extras = tables(triples, [small, *by_owner], virt_energy.reshape(1, T))

    mine = energy_of(triples, total[0], shares, others, *extras)
    everyone = lax.all_to_all(mine, "virt", 0, 0, tiled=True)
    return jnp.sum(everyone[:, 0, :T].reshape(4, 2, T), axis=0)


def solution(mesh):
    placed = (
        P("trip", "virt", None),
        P("trip", None, None, None, "virt"),
        P("trip", "virt", None),
        P("trip", None, "virt", None),
        P("trip", None, None),
        P("trip", None),
        P("trip"),
        P(),
        P("trip", None),
    )
    return jax.shard_map(
        local, mesh=mesh, in_specs=placed, out_specs=P("trip", None), check_vma=False
    )
```

```python
import functools

import jax
import jax.numpy as jnp
from jax import lax
from jax.experimental import pallas as pl
from jax.experimental.pallas import tpu as pltpu
from jax.sharding import PartitionSpec as P

T = 64
H = 32
F32 = jnp.float32
BF16 = jnp.bfloat16
CROWS = 16
BLOCK_ROWS = 2 * T + CROWS
SMALL_ROWS = 3 * H + 16
VMEM_LIMIT = 12 * 1024 * 1024


def shift_route(size, distance):
    return [(i, i + distance) for i in range(size) if 0 <= i + distance < size]


CORE_ROUTE = [(i, i ^ 1) for i in range(8)]


def in_hbm(array):
    return pltpu.with_memory_space_constraint(array, pltpu.HBM)


def lane_low(rows):
    return lax.broadcasted_iota(jnp.int32, (rows, 2 * T), 1) < T


def swap_halves(x):
    return pltpu.roll(x, T, 1)


def row_of(triples, owner, core, rel):
    s = jnp.where(core == 0, rel, 1 - rel)
    live = triples[s, 0] >= 0
    off_i = jnp.where(live, triples[s, 0] - owner, 2)
    off_j = jnp.where(live, triples[s, 1] - owner, 1)
    return off_i, off_j, live


def prep_kernel(triples, amps, coulomb, out1, out2, out3, up1, up2, blocks):
    owner, core = lax.axis_index("trip"), lax.rem(lax.axis_index("virt"), 2)
    occ_rows = coulomb.shape[1]
    for s in range(3):
        blocks[s, : 2 * T, :] = amps[s]
        turned = jnp.concatenate(
            [coulomb[s].astype(F32), jnp.zeros((T - occ_rows, T), F32)], axis=0
        ).T
        packed = jnp.concatenate([-turned[g * CROWS : (g + 1) * CROWS] for g in range(4)], axis=1)
        blocks[s, 2 * T :, :] = packed.astype(BF16)
    up1[...] = blocks[0:2]
    up2[...] = blocks[0]
    for rel in range(2):
        off_i, off_j, live = row_of(triples, owner, core, rel)
        for d, out in ((1, out1), (2, out2), (3, out3)):
            takes_part = live & ((off_i == d) | (off_j == d))
            other = jnp.clip(off_i + off_j - d - 1, 0, 2)

            @pl.when(takes_part)
            def _():
                out[rel] = blocks[other]

            @pl.when(jnp.logical_not(takes_part))
            def _():
                out[rel] = jnp.zeros((BLOCK_ROWS, 4 * T), BF16)


def prep(triples, amps, coulomb):
    vmem = pl.BlockSpec(memory_space=pltpu.VMEM)
    two = jax.ShapeDtypeStruct((2, BLOCK_ROWS, 4 * T), BF16)
    one = jax.ShapeDtypeStruct((BLOCK_ROWS, 4 * T), BF16)
    return pl.pallas_call(
        prep_kernel,
        out_shape=(two, two, two, two, one),
        in_specs=[pl.BlockSpec(memory_space=pltpu.SMEM), pl.BlockSpec(), pl.BlockSpec()],
        out_specs=[vmem] * 5,
        scratch_shapes=[
            pltpu.VMEM((3, BLOCK_ROWS, 4 * T), BF16),
        ],
        compiler_params=pltpu.CompilerParams(vmem_limit_bytes=VMEM_LIMIT),
        name="prep",
    )(triples, in_hbm(amps), in_hbm(coulomb))


STEPS = 8
DEPTH = 6 * T
PITCH = 2 * T + 8


def panels_kernel(integrals_in, holes, out, spread_a, spread_b, integrals, sems):
    occ_rows = holes.shape[0]
    per_step = H // STEPS
    width = per_step * 2 * T
    copies = []
    for step in range(STEPS):
        span = pl.ds(step * width, width)
        copies.append(
            pltpu.make_async_copy(integrals_in.at[:, span], integrals.at[:, span], sems.at[step])
        )
    for copy in copies:
        copy.start()
    for step in range(STEPS):
        copies[step].wait()
        for chunk in range(step * per_step, (step + 1) * per_step):
            columns = slice(chunk * 2 * T, (chunk + 1) * 2 * T)
            turned = integrals[:, columns].astype(F32).T
            for part in range(4):
                at = pl.ds((part % 2) * T + chunk * 2 + part // 2, H, stride=PITCH)
                spread_a[at, :] = turned[part * H : (part + 1) * H, : 2 * T]
                spread_b[at, :] = turned[part * H : (part + 1) * H, 2 * T :]
    for chunk in range(H):
        hole = holes[:, chunk * 2 * T : (chunk + 1) * 2 * T].astype(F32)
        hole = jnp.concatenate([hole, jnp.zeros((2 * T - occ_rows, 2 * T), F32)], axis=0).T
        for w in range(2):
            third = chunk * 2 + w
            at = third % H * 2 * T + third // H * T
            out[at : at + T, 4 * T :] = hole[w * T : (w + 1) * T].astype(BF16)

    def settle(step, _):
        rows = pl.ds(pl.multiple_of(step * 2 * T, 2 * T), 2 * T)
        source = pl.ds(pl.multiple_of(step * PITCH, 8), 2 * T)
        out[rows, : 2 * T] = spread_a[source, :].astype(BF16)
        out[rows, 2 * T : 4 * T] = spread_b[source, :].astype(BF16)
        return 0

    lax.fori_loop(0, H, settle, 0, unroll=32)


def panels_of(integrals, holes):
    return pl.pallas_call(
        panels_kernel,
        out_shape=jax.ShapeDtypeStruct((T * T, DEPTH), BF16),
        in_specs=[pl.BlockSpec(memory_space=pltpu.HBM), pl.BlockSpec()],
        out_specs=pl.BlockSpec(memory_space=pltpu.VMEM),
        scratch_shapes=[pltpu.VMEM(((H + 1) * PITCH, 2 * T), F32)] * 2
        + [
            pltpu.VMEM(integrals.shape, BF16),
            pltpu.SemaphoreType.DMA((STEPS,)),
        ],
        compiler_params=pltpu.CompilerParams(vmem_limit_bytes=VMEM_LIMIT),
        cost_estimate=pl.CostEstimate(flops=1 << 28, bytes_accessed=5 << 20, transcendentals=0),
        name="panels",
    )(in_hbm(integrals), in_hbm(holes))


def terms_kernel(rel, triples, got_one, got_two, in1, in2, in3, panels, out, chosen):
    core = lax.rem(lax.axis_index("virt"), 2)
    off_i, off_j, live = row_of(triples, lax.axis_index("trip"), core, rel)
    which = jnp.where(live, off_i + off_j - 3, 3)
    for at, option in enumerate((got_one.at[0], got_one.at[1], got_two)):

        @pl.when(which == at)
        def _():
            chosen[...] = option[...]

    @pl.when(which == 3)
    def _():
        chosen[...] = jnp.zeros_like(chosen)

    blocks = (chosen, in1.at[rel], in2.at[rel], in3.at[rel])
    lead, second = [], []
    for d in range(4):
        block = blocks[d][...]
        packed = block[2 * T :]
        coulomb = jnp.concatenate(
            [packed[:, g * T : (g + 1) * T] for g in range(4)], axis=0
        )
        coulomb = jnp.concatenate([coulomb, jnp.zeros_like(coulomb)], axis=1)
        lead.append(jnp.concatenate([block[:T], coulomb], axis=1))
        second.append(jnp.concatenate([block[T : 2 * T], coulomb], axis=1))
    lead = jnp.concatenate(lead, axis=0)
    second = jnp.concatenate(second, axis=0).astype(F32).T.astype(BF16)
    low = lane_low(T)
    contract = (((1,), (1,)), ((), ()))

    eighth = lax.broadcasted_iota(jnp.int32, (8, 2 * T), 1) // 8
    odd_eighth = jnp.bitwise_and(eighth, 1) == 1
    high_eighth = jnp.bitwise_and(eighth, 2) == 2

    def skewed(tile):
        result = []
        for half in range(2):
            rows = [tile[half * H + 8 * at : half * H + 8 * at + 8] for at in range(4)]
            rows = [jnp.where(odd_eighth, rows[(j - 1) % 4], rows[j]) for j in range(4)]
            result.append([jnp.where(high_eighth, rows[(j - 2) % 4], rows[j]) for j in range(4)])
        return result

    def group(step, _):
        panel = panels[pl.ds(pl.multiple_of(step * 8 * T, 8 * T), 8 * T), :]
        by_rows = jnp.dot(panel, second, preferred_element_type=F32)
        by_cols = lax.dot_general(lead, panel, contract, preferred_element_type=F32)

        def tiles_of(pair, duo):
            row = pair * 2 * T
            lanes = slice(duo * 2 * T, (duo + 1) * 2 * T)
            upper, lower = by_rows[row : row + T, lanes], by_rows[row + T : row + 2 * T, lanes]
            first = jnp.where(low, upper, swap_halves(lower))
            other = jnp.where(low, swap_halves(upper), lower)
            at = 2 * duo * T
            return (
                first + by_cols[at : at + T, row : row + 2 * T],
                other + by_cols[at + T : at + 2 * T, row : row + 2 * T],
            )

        for two in range(2):
            evens = tiles_of(2 * two, 0) + tiles_of(2 * two, 1)
            odds = tiles_of(2 * two + 1, 0) + tiles_of(2 * two + 1, 1)
            at = pl.ds(pl.multiple_of((step * 4 + 2 * two) * 8, 16), 16)
            for d, (even, odd) in enumerate(zip(evens, odds)):
                if d == 0:
                    tiles = [
                        skewed(jnp.where(low, even, swap_halves(odd))),
                        skewed(jnp.where(low, swap_halves(even), odd)),
                    ]
                else:
                    first, second_tile = skewed(even), skewed(odd)
                    tiles = [(first[half], second_tile[half]) for half in range(2)]
                for half in range(2):
                    for j in range(4):
                        part = lax.rem(step // 2 + j, 4)
                        index = part * 4 + d if half == 0 else d * 4 + part
                        rows16 = jnp.concatenate([tiles[half][0][j], tiles[half][1][j]], axis=0)
                        out[half, index, at, :] = rows16.astype(BF16)
        return 0

    lax.fori_loop(0, 8, group, 0, unroll=8)


def terms(rel, triples, blocks, panels):
    vmem = pl.BlockSpec(memory_space=pltpu.VMEM)
    return pl.pallas_call(
        functools.partial(terms_kernel, rel),
        out_shape=jax.ShapeDtypeStruct((2, 16, 256, 2 * T), BF16),
        in_specs=[pl.BlockSpec(memory_space=pltpu.SMEM)] + [vmem] * 6,
        out_specs=vmem,
        scratch_shapes=[pltpu.VMEM((BLOCK_ROWS, 4 * T), BF16)],
        compiler_params=pltpu.CompilerParams(vmem_limit_bytes=VMEM_LIMIT),
        cost_estimate=pl.CostEstimate(flops=1 << 31, bytes_accessed=5 << 20, transcendentals=0),
        name="terms",
    )(triples, *blocks, panels)


def add_kernel(keep, got, exchange, singles, occ, first, own, one, two, three, small, table):
    for s in range(3):
        for row in range(H):
            lanes = slice(row * 2 * T, (row + 1) * 2 * T)
            table[s * H + row : s * H + row + 1, :] = exchange[s : s + 1, lanes].astype(F32)
    heads = [singles[...].astype(F32), jnp.broadcast_to(occ[...].astype(F32), (1, T))]
    table[3 * H :, :] = jnp.broadcast_to(jnp.concatenate(heads, axis=1), (16, 2 * T))
    small[...] = table[...].astype(BF16)
    second = (own, one, two, three)
    for half, outs in ((0, [first]), (1, second)):
        per_out = 16 // len(outs)
        for at, out in enumerate(outs):

            def one(index, _):
                source = at * per_out + index
                total = keep[half, source].astype(F32) + got[half, source].astype(F32)
                out[pl.ds(pl.multiple_of(index * 256, 256), 256), :] = total.astype(BF16)
                return 0

            lax.fori_loop(0, per_out, one, 0, unroll=4)
    for out in second[1:]:
        out[1024:, :] = small[...]


def add(keep, got, exchange, singles, occ):
    vmem = pl.BlockSpec(memory_space=pltpu.VMEM)

    def rows(count):
        return jax.ShapeDtypeStruct((count, 2 * T), BF16)

    return pl.pallas_call(
        add_kernel,
        out_shape=(rows(4096), rows(1024))
        + (rows(1024 + SMALL_ROWS),) * 3
        + (rows(SMALL_ROWS),),
        in_specs=[vmem] * 5,
        out_specs=[vmem] * 6,
        scratch_shapes=[pltpu.VMEM((SMALL_ROWS, 2 * T), F32)],
        compiler_params=pltpu.CompilerParams(vmem_limit_bytes=VMEM_LIMIT),
        name="add",
    )(keep, got, exchange, singles, occ)


def collect_kernel(by_y, out):
    for d in range(4):
        out[d] = sum(by_y[source * 4 + d].astype(F32) for source in range(4))


def collect(by_y):
    vmem = pl.BlockSpec(memory_space=pltpu.VMEM)
    return pl.pallas_call(
        collect_kernel,
        out_shape=jax.ShapeDtypeStruct((4, 256, 2 * T), F32),
        in_specs=[vmem],
        out_specs=vmem,
        compiler_params=pltpu.CompilerParams(vmem_limit_bytes=VMEM_LIMIT),
        name="collect",
    )(by_y)


def gather_terms(mid_is_j, one, two, three, by_j, by_i):
    middle = two.astype(F32)
    rows = slice(0, one.shape[0])
    by_j[rows, :] = one.astype(F32) + jnp.where(mid_is_j, middle, 0.0)
    by_i[rows, :] = three.astype(F32) + jnp.where(mid_is_j, 0.0, middle)


def lane_key(part, rows, lanes):
    quarter = lax.broadcasted_iota(jnp.int32, (rows, lanes), 1) // 8
    return jnp.bitwise_and(part + 4 * 64 - quarter, 3)


def by_key(key, options, shift):
    value = options[(3 - shift) % 4]
    for k in (2, 1, 0):
        value = jnp.where(key == k, options[(k - shift) % 4], value)
    return value


def own_tile(load, key, q):
    groups = []
    pairs = [load((c_quarter * 4 + q) * 16).astype(F32) for c_quarter in range(4)]
    for half in range(2):
        options = [x[half * 8 : half * 8 + 8] for x in pairs]
        groups += [by_key(key, options, b_quarter) for b_quarter in range(4)]
    return jnp.concatenate(groups, axis=0)


def turned_sums(owns, by_j, by_i, base, q):
    low, low_rows = lane_low(H), lane_low(T)

    def as_rows(table, q):
        even = table[pl.ds(base + 2 * q, H, stride=8), :]
        odd = table[pl.ds(base + 2 * q + 1, H, stride=8), :]
        top = jnp.where(low, even, swap_halves(odd))
        bottom = jnp.where(low, swap_halves(even), odd)
        return jnp.concatenate([top, bottom], axis=0)

    flat = jnp.concatenate([as_rows(by_i, q), as_rows(by_i, q + 1)], axis=0).T
    first, second = flat[:T], flat[T:]
    return (
        owns[0] + as_rows(by_j, q) + jnp.where(low_rows, first, swap_halves(second)),
        owns[1] + as_rows(by_j, q + 1) + jnp.where(low_rows, swap_halves(first), second),
    )


def middle_is_j(triples):
    core = lax.rem(lax.axis_index("virt"), 2)
    _, off_j, _ = row_of(triples, lax.axis_index("trip"), core, 0)
    return off_j == 2


def combine_kernel(triples, own, one, two, three, out, by_j, by_i):
    rows = pl.ds(0, 1024)
    gather_terms(middle_is_j(triples), one[rows, :], two[rows, :], three[rows, :], by_j, by_i)
    for part in range(4):
        key = lane_key(part, 8, 2 * T)

        def load(at):
            return own[part * 256 + at : part * 256 + at + 16, :]

        for q in (0, 2):
            owns = [own_tile(load, key, q), own_tile(load, key, q + 1)]
            for at, total in enumerate(turned_sums(owns, by_j, by_i, part * 256, q)):
                out[part, (q + at) * T : (q + at + 1) * T, :] = total.astype(BF16)


def combine(triples, own, one, two, three):
    vmem = pl.BlockSpec(memory_space=pltpu.VMEM)
    return pl.pallas_call(
        combine_kernel,
        out_shape=jax.ShapeDtypeStruct((4, 256, 2 * T), BF16),
        in_specs=[pl.BlockSpec(memory_space=pltpu.SMEM)] + [vmem] * 4,
        out_specs=vmem,
        scratch_shapes=[pltpu.VMEM((1024 + 8, 2 * T), F32)] * 2,
        compiler_params=pltpu.CompilerParams(vmem_limit_bytes=VMEM_LIMIT),
        name="combine",
    )(triples, own, one, two, three)


PART_PITCH = T + 8
PART_ROWS = 17 * PART_PITCH


def energy_kernel(
    triples, own, one, two, three, others, extra_b, extra_a, inverse, out, by_j, by_i, plain, turned
):
    virt = lax.axis_index("virt")
    _, _, live = row_of(triples, lax.axis_index("trip"), lax.rem(virt, 2), 0)
    gather_terms(middle_is_j(triples), one[...], two[...], three[...], by_j, by_i)
    wide_key = lane_key(virt // 2, 8, 2 * T)
    key = lane_key(virt // 2, 8, T)
    for q in range(4):
        if q % 2 == 0:
            owns = [own_tile(lambda at: own[at : at + 16, :], wide_key, q + at) for at in range(2)]
            firsts = turned_sums(owns, by_j, by_i, 0, q)
        first = firsts[q % 2]
        at = slice(q * T, (q + 1) * T)
        second = sum(others[source, at, :].astype(F32) for source in range(4))
        flat = jnp.concatenate([first, second], axis=0).T
        flat_swapped = swap_halves(flat)
        for half, tile, across in ((0, first, flat), (1, second, flat_swapped)):
            base = (half * 8 + 2 * q) * PART_PITCH
            plain[base : base + T, :] = tile[:, :T]
            turned[base : base + T, :] = across[:T, :T]
            base += PART_PITCH
            plain[base : base + T, :] = swap_halves(tile)[:, :T]
            turned[base : base + T, :] = across[T:, :T]

    def exchanged(table, half, c_low):
        groups = []
        for b_half in range(2):
            options = [
                table[
                    pl.ds(b_half * 8 * PART_PITCH + half * H + 8 * at + c_low, 8, stride=PART_PITCH), :
                ]
                for at in range(4)
            ]
            groups += [by_key(key, options, b_quarter) for b_quarter in range(4)]
        return jnp.concatenate(groups, axis=0)

    sum_b = jnp.zeros((T, T), F32)
    sum_a = jnp.zeros((T, T), F32)
    for c_low in range(8):
        acbs = [exchanged(plain, half, c_low) for half in range(2)]
        flat = jnp.concatenate(acbs, axis=1).T
        for half, acb in enumerate(acbs):
            index = half * 8 + c_low
            at = slice(index * T, (index + 1) * T)
            cab = exchanged(turned, half, c_low)
            bca = flat[half * T : (half + 1) * T]
            bac = turned[index * PART_PITCH : index * PART_PITCH + T, :]
            inv = inverse[at, :]
            sum_b += (4.0 * bac + acb) * (bac - cab + extra_b[at, :]) * inv
            sum_a += bac * (acb - bca + extra_a[at, :]) * inv
    total = jnp.sum(sum_a + sum_b.T, axis=0, keepdims=True)
    total = jnp.where(live, total, 0.0)
    total = jnp.concatenate([total, jnp.zeros_like(total)], axis=1)
    out[...] = jnp.broadcast_to(total[None], out.shape)


def energy_of(triples, own, shares, others, extra_b, extra_a, inverse):
    vmem = pl.BlockSpec(memory_space=pltpu.VMEM)
    return pl.pallas_call(
        energy_kernel,
        out_shape=jax.ShapeDtypeStruct((8, 8, 2 * T), F32),
        in_specs=[pl.BlockSpec(memory_space=pltpu.SMEM)] + [vmem] * 8,
        out_specs=vmem,
        scratch_shapes=[pltpu.VMEM((256 + 8, 2 * T), F32)] * 2 + [pltpu.VMEM((PART_ROWS, T), F32)] * 2,
        compiler_params=pltpu.CompilerParams(vmem_limit_bytes=VMEM_LIMIT),
        name="energy",
    )(triples, own, *shares, others, extra_b, extra_a, inverse)


def tables_kernel(
    triples, own, one, two, three, virt_energy, extra_b, extra_a, inverse, columns, rows, matrices
):
    virt = lax.axis_index("virt")
    off_i, off_j, _ = row_of(triples, lax.axis_index("trip"), lax.rem(virt, 2), 0)
    part = virt // 2

    def small_of(table):
        return table[table.shape[0] - SMALL_ROWS :, :]

    def exch(slot, table, index):
        flat = small_of(table)[index * H : (index + 1) * H, :].astype(F32)
        matrices[pl.ds(slot * T, H, stride=2), :] = flat[:, :T]
        matrices[pl.ds(slot * T + 1, H, stride=2), :] = swap_halves(flat)[:, :T]
        return matrices[slot * T : (slot + 1) * T, :]

    def pick(options, index):
        result = options[-1]
        for at in range(len(options) - 1):
            result = jnp.where(index == at, options[at], result)
        return result

    own_exch = [exch(slot, own, slot) for slot in range(3)]
    kj = pick(own_exch[:2], off_j - 1)
    ki = pick(own_exch[1:], off_i - 2)
    ji = pick([exch(3, one, 0), exch(4, one, 1), exch(5, two, 0)], off_i + off_j - 3)
    kj_t, ki_t, ji_t = kj.T, ki.T, ji.T
    heads = [small_of(x)[3 * H :, :].astype(F32) for x in (own, one, two, three)]
    head_i = pick([heads[2], heads[3]], off_i - 2)
    head_j = pick([heads[1], heads[2]], off_j - 1)
    head_k = heads[0]
    occ = head_i[0:1, T:] + head_j[0:1, T:] + head_k[0:1, T:]
    s_i, s_j, s_k = (x[0:1, :T] for x in (head_i, head_j, head_k))
    e_a = virt_energy[...]
    s_ib, s_jb, s_kb, e_b = (jnp.broadcast_to(v, (T, T)).T for v in (s_i, s_j, s_k, e_a))
    for at, m in enumerate((kj, ji_t, ji, kj_t, s_ib, s_jb, s_kb, e_b)):
        rows[at * T : (at + 1) * T, :] = m
    for at, m in enumerate((kj, ji_t, ki_t, ki)):
        for half in range(2):
            for quarter in range(4):
                base = quarter * T + at * 16 + half * 8
                source = half * H + quarter * 8
                columns[base : base + 8, :] = m[source : source + 8]
    key = lane_key(part, 1, T)
    key_rows = lane_key(part, T, T)
    c_of_row = lax.broadcasted_iota(jnp.int32, (T, T), 0)
    ki_diff = ki - ki_t

    def one(index, _):
        half, c_low = index // 8, lax.rem(index, 8)
        first_c = half * H + c_low
        looked_up = [
            [rows[pl.ds(at * T + first_c + 8 * quarter, 1), :] for quarter in range(4)]
            for at in range(8)
        ]
        for quarter in range(4):
            wanted = first_c + 8 * jnp.bitwise_and(key_rows - quarter, 3)
            choice = jnp.where(c_of_row == wanted, 1.0, 0.0).astype(BF16)
            source = columns[quarter * T : (quarter + 1) * T, :].astype(BF16)
            over_bc = jnp.dot(source, choice, preferred_element_type=F32)
            kj_ca, ji_ac, ji_ca, kj_ac, si_c, sj_c, sk_c, e_c = (
                by_key(key, options, quarter) for options in looked_up
            )
            for b_half in range(2):
                at = b_half * H + quarter * 8
                b = slice(at, at + 8)
                kj_bc, ji_cb, ki_cb, ki_bc = (
                    over_bc[g * 16 + b_half * 8 : g * 16 + b_half * 8 + 8] for g in range(4)
                )
                target = pl.ds(pl.multiple_of(index * T + at, 8), 8)
                extra_b[target, :] = (
                    s_ib[b] * kj_ca
                    - s_kb[b] * ji_ac
                    + s_j * (ki_cb - ki_bc)
                    + sk_c * ji_t[b]
                    - si_c * kj[b]
                )
                extra_a[target, :] = (
                    s_kb[b] * ji_ca
                    - s_ib[b] * kj_ac
                    + s_i * kj_bc
                    - s_k * ji_cb
                    + sj_c * ki_diff[b]
                )
                inverse[target, :] = 1.0 / (occ - e_a - e_b[b] - e_c)
        return 0

    lax.fori_loop(0, 16, one, 0, unroll=2)


def tables(triples, small, virt_energy):
    vmem = pl.BlockSpec(memory_space=pltpu.VMEM)
    table = jax.ShapeDtypeStruct((16 * T, T), F32)
    return pl.pallas_call(
        tables_kernel,
        out_shape=(table, table, table),
        in_specs=[pl.BlockSpec(memory_space=pltpu.SMEM)] + [vmem] * 5,
        out_specs=[vmem] * 3,
        scratch_shapes=[pltpu.VMEM((rows * T + 8, T), F32) for rows in (4, 8, 6)],
        compiler_params=pltpu.CompilerParams(vmem_limit_bytes=VMEM_LIMIT),
        cost_estimate=pl.CostEstimate(flops=1 << 28, bytes_accessed=3 << 20, transcendentals=0),
        name="tables",
    )(triples, *small, virt_energy)


def local(
    virt_integrals,
    pair_amps,
    hole_amps,
    coulomb_ints,
    exchange_ints,
    singles,
    occ_energy,
    virt_energy,
    triples,
):
    n_trip = lax.axis_size("trip")

    out1, out2, out3, up1, up2 = prep(
        triples, pair_amps.reshape(3, 2 * T, 4 * T), coulomb_ints.reshape(coulomb_ints.shape[1:])
    )
    got_two = lax.ppermute(up2, "trip", shift_route(n_trip, -2))
    in2 = lax.ppermute(out2, "trip", shift_route(n_trip, 2))
    got_one = lax.ppermute(up1, "trip", shift_route(n_trip, -1))
    in1 = lax.ppermute(out1, "trip", shift_route(n_trip, 1))
    in3 = lax.ppermute(out3, "trip", shift_route(n_trip, 3))
    blocks = (got_one, got_two, in1, in2, in3)

    panels = panels_of(
        virt_integrals.reshape(4 * T, T * T), hole_amps.reshape(hole_amps.shape[1:])
    )

    send = terms(1, triples, blocks, panels)
    got = lax.ppermute(send, "virt", CORE_ROUTE)
    keep = terms(0, triples, blocks, panels)
    first_half, *second_half, small = add(
        keep, got, exchange_ints.reshape(3, T * T), singles, occ_energy.reshape(1, 1)
    )
    over_y = functools.partial(
        lax.all_to_all,
        axis_name="virt",
        split_axis=0,
        concat_axis=0,
        axis_index_groups=[[0, 2, 4, 6], [1, 3, 5, 7]],
        tiled=True,
    )
    by_y = over_y(first_half.reshape(16, 256, 2 * T))
    by_owner = [
        lax.ppermute(second_half[d], "trip", shift_route(n_trip, -d)) for d in (1, 2, 3)
    ]

    total = collect(by_y)
    to_share = [total[d].astype(BF16) for d in (1, 2, 3)]
    shares = [
        lax.ppermute(to_share[d - 1], "trip", shift_route(n_trip, -d)) for d in (1, 2, 3)
    ]
    by_owner, _ = lax.optimization_barrier((by_owner, to_share))
    others = over_y(combine(triples, second_half[0], *by_owner))
    extras = tables(triples, [small, *by_owner], virt_energy.reshape(1, T))

    mine = energy_of(triples, total[0], shares, others, *extras)
    everyone = lax.all_to_all(mine, "virt", 0, 0, tiled=True)
    return jnp.sum(everyone[:, 0, :T].reshape(4, 2, T), axis=0)


def solution(mesh):
    placed = (
        P("trip", "virt", None),
        P("trip", None, None, None, "virt"),
        P("trip", "virt", None),
        P("trip", None, "virt", None),
        P("trip", None, None),
        P("trip", None),
        P("trip"),
        P(),
        P("trip", None),
    )
    return jax.shard_map(
        local, mesh=mesh, in_specs=placed, out_specs=P("trip", None), check_vma=False
    )
```
